512 devices in a mesh: wide: 64 (over y, z), narrow: 8 (over x, core).
Axes of the slice: x: 4, y: 8, z: 8, core: 2. Of those that a mesh axis runs over, the one named last changes fastest.
Arguments:
- right_side: float32 [8, 2048, 1024], P(None, 'wide', 'narrow'), may hold values from -6 to 6
- wet_mask: int32 [8, 2048, 1024], P(None, 'wide', 'narrow'), may hold values 0 or 1
- helmholtz: float32 [8, 2048, 1024], P(None, 'wide', 'narrow'), may hold values from 0.02 to 2
- eig_low: float32 [1], replicated, may hold values from 0.03 to 0.3
- eig_high: float32 [1], replicated, may hold values from 1.6 to 2
Outputs:
- pressure: float32 [8, 2048, 1024], P(None, 'wide', 'narrow')
- residual: float32 [8, 2048, 1024], P(None, 'wide', 'narrow')
The draws below stay inside these ranges and needn't reach their ends.
All inputs are finite; a program needn't handle non-finite values. No bound on the sum of `wet_mask` on one device may be relied on, other than what follows from the above.
Results may differ from the reference program's by a relative error of at most 0.000044.
Values sent between devices are 32-bit elements; how exact they have to be, the bound alone decides.
No kernel may reach another device: no remote copies, remote signals or barrier semaphores. Data moves between devices by JAX's collectives and lax.ppermute only.
A program may use at most 64 MiB of HBM per device.

```python
import math
import jax
import jax.numpy as jnp
from jax import lax

CZ = 8
PRE = 2
POST = 2
CHEB = 4
NX = 2048
NY = 1024


def touch_ends(entries, own_key, least, top_value):
    spot = [jax.random.randint(jax.random.fold_in(own_key, axis), (), 0, length) for axis, length in enumerate(entries.shape)]
    main_axis = entries.shape.index(max(entries.shape))
    beside = spot[:main_axis] + [(spot[main_axis] + 1) % entries.shape[main_axis]] + spot[main_axis + 1:]
    return entries.at[tuple(spot)].set(least).at[tuple(beside)].set(top_value)


def block_levels(stream_key, extent, pieces, low, high):
    def one(axis_at, parts):
        draws = jax.random.uniform(jax.random.fold_in(jax.random.fold_in(stream_key, 6), axis_at), (parts,), jnp.float32, low / len(pieces), high / len(pieces))
        return jnp.repeat(jnp.exp(draws), extent[axis_at] // parts).reshape((-1,) + (1,) * (len(extent) - axis_at - 1))

    gain = one(*pieces[0])
    for cut in pieces[1:]:
        gain = gain * one(*cut)
    return gain


def centred(rng, dims, spread, bound, pieces=(), kind=jnp.bfloat16):
    drawn = jax.random.normal(rng, dims, jnp.float32) * spread
    if len(pieces) > 0:
        drawn = block_levels(rng, dims, pieces, -0.22, 0.18) * drawn
    return jnp.clip(drawn, min=-bound, max=bound).astype(kind)


def setup_inputs(seed: int = 0) -> dict:
    key_of = jax.random.split(jax.random.key(seed), 6)
    right_side = centred(key_of[0], (CZ, NX, NY), 1.0, 6.0, ((1, 64), (2, 8)), jnp.float32)
    wet_mask = touch_ends((jax.random.randint(key_of[1], (CZ, NX, NY), 0, 4) < 3).astype(jnp.int32), jax.random.fold_in(key_of[1], 1), 0, 1)
    helmholtz = jnp.clip(jnp.exp(math.log(2.0) - 4.6051702 * jax.random.uniform(key_of[2], (CZ, NX, NY), jnp.float32) ** block_levels(key_of[2], (CZ, NX, NY), ((1, 64), (2, 8)), -0.2, 0.2)), 0.02, 2.0)
    eig_low = jnp.clip(jax.random.uniform(key_of[3], (1,), jnp.float32, 0.03, 0.3), 0.03, 0.3)
    eig_high = jnp.clip(jax.random.uniform(key_of[4], (1,), jnp.float32, 1.6, 2.0), 1.6, 2.0)
    return dict(right_side=right_side, wet_mask=wet_mask, helmholtz=helmholtz, eig_low=eig_low, eig_high=eig_high)


def neighbours(padded):
    total = padded[2:, 1:-1, 1:-1] + padded[:-2, 1:-1, 1:-1]
    total = total + padded[1:-1, 2:, 1:-1] + padded[1:-1, :-2, 1:-1]
    total = total + padded[1:-1, 1:-1, 2:] + padded[1:-1, 1:-1, :-2]
    return total


def pad_vertical(field):
    return jnp.pad(field, ((1, 1), (0, 0), (0, 0)))


def pad_sides(field):
    return jnp.pad(field, ((0, 0), (1, 1), (1, 1)))


def coarsen(field):
    first, second, third = field.shape
    blocks = field.reshape(first // 2, 2, second // 2, 2, third // 2, 2)
    return jnp.sum(blocks, axis=(1, 3, 5)) * 0.125


def refine_axis(field, axis):
    length = field.shape[axis] - 2
    centre = lax.slice_in_dim(field, 1, length + 1, axis=axis)
    before = lax.slice_in_dim(field, 0, length, axis=axis)
    after = lax.slice_in_dim(field, 2, length + 2, axis=axis)
    low_half = 0.75 * centre + 0.25 * before
    high_half = 0.75 * centre + 0.25 * after
    stacked = jnp.stack((low_half, high_half), axis=axis + 1)
    shape = list(centre.shape)
    shape[axis] = 2 * length
    return stacked.reshape(shape)


def refine(padded):
    field = refine_axis(padded, 1)
    field = refine_axis(field, 2)
    return refine_axis(pad_vertical(field), 0)


def coarse_apply(field, wet_c, shift_c, count_c):
    near = neighbours(pad_vertical(pad_sides(wet_c * field)))
    return wet_c * ((shift_c + 0.25 * count_c) * field - 0.25 * near) + (1.0 - wet_c) * field


def chebyshev(source, wet_c, shift_c, count_c, low_bound, high_bound):
    centre_value = 0.5 * (high_bound + low_bound)
    half_width = 0.5 * (high_bound - low_bound)
    sigma_value = centre_value / half_width
    rho_value = 1.0 / sigma_value
    diag_c = wet_c * (shift_c + 0.25 * count_c) + (1.0 - wet_c)
    remain = source
    direction = remain / diag_c / centre_value
    error_c = jnp.zeros_like(source)
    for sweep in range(CHEB):
        error_c = error_c + direction
        if sweep + 1 < CHEB:
            remain = remain - coarse_apply(direction, wet_c, shift_c, count_c)
            rho_next = 1.0 / (2.0 * sigma_value - rho_value)
            direction = rho_next * rho_value * direction + (2.0 * rho_next / half_width) * remain / diag_c
            rho_value = rho_next
    return error_c


def reference(right_side, wet_mask, helmholtz, eig_low, eig_high):
    wet = wet_mask.astype(jnp.float32)
    count = neighbours(pad_vertical(pad_sides(wet)))
    fine_diag = wet * (helmholtz + count) + (1.0 - wet)

    def fine_apply(field):
        near = neighbours(pad_vertical(pad_sides(wet * field)))
        return wet * ((helmholtz + count) * field - near) + (1.0 - wet) * field

    pressure = jnp.zeros_like(right_side)
    for sweep in range(PRE):
        pressure = pressure + 0.8 * (right_side - fine_apply(pressure)) / fine_diag
    fine_res = right_side - fine_apply(pressure)
    coarse_src = coarsen(wet * fine_res)
    first, second, third = wet_mask.shape
    wet_sum = jnp.sum(wet_mask.reshape(first // 2, 2, second // 2, 2, third // 2, 2), axis=(1, 3, 5))
    wet_c = (wet_sum >= 4).astype(jnp.float32)
    shift_c = wet_c * coarsen(helmholtz)
    count_c = neighbours(pad_vertical(pad_sides(wet_c)))
    error_c = chebyshev(coarse_src, wet_c, shift_c, count_c, eig_low[0], eig_high[0])
    pressure = pressure + wet * refine(pad_sides(error_c))
    for sweep in range(POST):
        pressure = pressure + 0.8 * (right_side - fine_apply(pressure)) / fine_diag
    residual = right_side - fine_apply(pressure)
    return pressure, residual
```

```python
import functools

import jax
import jax.numpy as jnp
from jax import lax
from jax.experimental import pallas as pl
from jax.experimental.pallas import tpu as pltpu
from jax.sharding import PartitionSpec as P

CHEB = 4

CZ = 8
ROWS = 32
LANES = 128
RIM = 14
TALL = ROWS + 2 * RIM
MASK_RIM = 13
RIGHT_RIM = 12
STRIP = MASK_RIM + 2 * RIGHT_RIM
SIDE = 16
GROUP = LANES // SIDE
PACKED = 8
WIDE = 2 * LANES

VMEM = pl.BlockSpec(memory_space=pltpu.VMEM)
SMEM = pl.BlockSpec(memory_space=pltpu.SMEM)


def brick_row(ref, row):
    return ref[pl.ds(row, CZ, stride=ROWS), :]


def strips_kernel(right_ref, mask_ref, helm_ref, first_ref, last_ref):
    for out_ref, mask_from, other_from in (
        (first_ref, 0, 0),
        (last_ref, ROWS - MASK_RIM, ROWS - RIGHT_RIM),
    ):
        for row in range(MASK_RIM):
            out_ref[row] = brick_row(mask_ref, mask_from + row).astype(jnp.float32)
        for row in range(RIGHT_RIM):
            out_ref[MASK_RIM + row] = brick_row(helm_ref, other_from + row)
            out_ref[MASK_RIM + RIGHT_RIM + row] = brick_row(right_ref, other_from + row)


def sides_kernel(
    right_ref, mask_ref, helm_ref, before_ref, after_ref, tall_ref, first_ref, last_ref
):
    zero = jnp.zeros((CZ, LANES), jnp.float32)
    for field in range(3):
        for row in (0, 1, TALL - 2, TALL - 1):
            tall_ref[field, row] = zero
    for field, own_ref, offset, rim in (
        (0, mask_ref, 0, MASK_RIM),
        (1, helm_ref, MASK_RIM, RIGHT_RIM),
        (2, right_ref, MASK_RIM + RIGHT_RIM, RIGHT_RIM),
    ):
        for row in range(rim):
            tall_ref[field, RIM - rim + row] = before_ref[offset + row]
            tall_ref[field, RIM + ROWS + row] = after_ref[offset + row]
        for row in range(ROWS):
            tall_ref[field, RIM + row] = brick_row(own_ref, row).astype(jnp.float32)
    lane = lax.broadcasted_iota(jnp.int32, (CZ, LANES), 1)
    for field in range(3):

        def pack(group, carry):
            first, last = zero, zero
            for k in range(GROUP):
                line = tall_ref[field, jnp.minimum(group * GROUP + k, TALL - 1)]
                here = (lane >= SIDE * k) & (lane < SIDE * (k + 1))
                one = pltpu.roll(line, SIDE * k, 1) if k else line
                two = pltpu.roll(line, (SIDE * (k + 1)) % LANES, 1) if k + 1 < GROUP else line
                first = jnp.where(here, one, first)
                last = jnp.where(here, two, last)
            first_ref[field * PACKED + group] = first
            last_ref[field * PACKED + group] = last
            return carry

        lax.fori_loop(0, PACKED, pack, 0)


def rows_loop(start, stop, chunk, step):
    count = (stop - start) // chunk
    assert count * chunk == stop - start

    def body(index, carry):
        step(start + index * chunk)
        return carry

    lax.fori_loop(0, count, body, 0)


def cycle_kernel(
    eig_low_ref,
    eig_high_ref,
    tall_ref,
    left_ref,
    right_ref,
    pressure_ref,
    residual_ref,
    wet,
    helm,
    rhs,
    diag,
    base,
    gain,
    flow,
    flow_next,
    state,
    wet_c,
    diag_c,
    inverse_c,
    remain,
    error,
    direction,
    masked,
    masked_next,
):
    lane = lax.broadcasted_iota(jnp.int32, (CZ, LANES), 1)

    for field, dest in ((0, wet), (1, helm), (2, rhs)):

        def unpack(group, carry):
            after = right_ref[field * PACKED + group]
            ahead = pltpu.roll(left_ref[field * PACKED + group], LANES - SIDE, 1)
            for k in range(GROUP):
                row = jnp.minimum(group * GROUP + k, TALL - 1)
                low, high = SIDE * k, SIDE * (k + 1)
                beyond = (low - SIDE) % LANES
                both = jnp.where((lane >= beyond) & (lane < beyond + SIDE), ahead, 0.0)
                both = jnp.where((lane >= low) & (lane < high), after, both)
                if k:
                    both = pltpu.roll(both, LANES - low, 1)
                dest[row, :, :LANES] = tall_ref[field, row]
                dest[row, :, LANES:] = both
            return carry

        lax.fori_loop(0, PACKED, unpack, 0)

    def planes(count):
        level = lax.broadcasted_iota(jnp.int32, (count, CZ, WIDE), 1)
        column = lax.broadcasted_iota(jnp.int32, (count, CZ, WIDE), 2)
        return level, column

    def near_rows(ref, row, count, reach, ahead=1):
        level, _ = planes(count)
        here = ref[pl.ds(row, count)]
        total = ref[pl.ds(row - 1, count)] + ref[pl.ds(row + 1, count)]
        total = total + jnp.where(level >= reach, pltpu.roll(here, reach, 1), 0.0)
        total = total + jnp.where(level < CZ - reach, pltpu.roll(here, CZ - reach, 1), 0.0)
        return total + (pltpu.roll(here, reach, 2) + pltpu.roll(here, WIDE - reach, 2))

    def smooth_setup(row, chunk=4):
        rows = pl.ds(row, chunk)
        water = wet[rows]
        count = near_rows(wet, row, chunk, 1)
        scale = water * (helm[rows] + count) + (1.0 - water)
        inverse = 0.8 / scale
        start = inverse * rhs[rows]
        diag[rows] = scale
        base[rows] = start
        gain[rows] = inverse * water
        flow[rows] = water * start

    rows_loop(2, 58, 4, smooth_setup)

    def smooth_second(row, chunk=3):
        rows = pl.ds(row, chunk)
        value = 1.2 * base[rows] + gain[rows] * near_rows(flow, row, chunk, 1)
        state[rows] = value
        flow_next[rows] = wet[rows] * value

    rows_loop(3, 57, 3, smooth_second)

    def pair_sum(value):
        level, column = planes(value.shape[0])
        other = jnp.where(
            level % 2 == 0, pltpu.roll(value, CZ - 1, 1), pltpu.roll(value, 1, 1)
        )
        value = value + other
        other = jnp.where(
            column % 2 == 0, pltpu.roll(value, WIDE - 1, 2), pltpu.roll(value, 1, 2)
        )
        return value + other

    def coarse_mask(row, chunk=4):
        total = jnp.stack([wet[2 * (row + i)] + wet[2 * (row + i) + 1] for i in range(chunk)])
        wet_c[pl.ds(row, chunk)] = jnp.where(pair_sum(total) >= 3.5, 1.0, 0.0)

    rows_loop(1, 29, 4, coarse_mask)

    low = jnp.full((1, CZ, WIDE), eig_low_ref[0], jnp.float32)
    high = jnp.full((1, CZ, WIDE), eig_high_ref[0], jnp.float32)
    centre = 0.5 * (high + low)
    half = 0.5 * (high - low)
    sigma = centre / half
    rho = 1.0 / sigma
    start_scale = 1.0 / centre

    def coarse_setup(row, chunk=2):
        rows = pl.ds(row, chunk)
        fine = pl.ds(2 * row, 2 * chunk)
        water = wet[fine]
        left_over = water * (
            rhs[fine] - diag[fine] * state[fine] + near_rows(flow_next, 2 * row, 2 * chunk, 1)
        )
        lumps = helm[fine]
        source = jnp.stack([left_over[2 * i] + left_over[2 * i + 1] for i in range(chunk)])
        shift = jnp.stack([lumps[2 * i] + lumps[2 * i + 1] for i in range(chunk)])
        source = 0.125 * pair_sum(source)
        shift = 0.125 * pair_sum(shift)
        water_c = wet_c[rows]
        count_c = near_rows(wet_c, row, chunk, 2)
        scale = water_c * (shift + 0.25 * count_c) + (1.0 - water_c)
        inverse = 1.0 / scale
        first = source * inverse * start_scale
        diag_c[rows] = scale
        inverse_c[rows] = inverse
        remain[rows] = source
        error[rows] = first
        direction[rows] = first
        masked[rows] = water_c * first

    rows_loop(2, 28, 2, coarse_setup)

    source_ref, other_ref = masked, masked_next
    for sweep in range(1, CHEB):
        rho_next = 1.0 / (2.0 * sigma - rho)
        keep = rho_next * rho
        add = 2.0 * rho_next / half

        def chebyshev(row, chunk=2, keep=keep, add=add, now=source_ref, later=other_ref):
            rows = pl.ds(row, chunk)
            old = direction[rows]
            water_c = wet_c[rows]
            left_over = remain[rows] - (
                diag_c[rows] * old - 0.25 * water_c * near_rows(now, row, chunk, 2)
            )
            fresh = keep * old + add * (left_over * inverse_c[rows])
            remain[rows] = left_over
            direction[rows] = fresh
            error[rows] = error[rows] + fresh
            later[rows] = water_c * fresh

        rows_loop(2 + sweep, 28 - sweep, 2, chebyshev)
        rho = rho_next
        source_ref, other_ref = other_ref, source_ref

    def spread(row, chunk=2):
        level, column = planes(chunk)
        value = error[pl.ds(row, chunk)]
        other = jnp.where(
            column % 2 == 0, pltpu.roll(value, 1, 2), pltpu.roll(value, WIDE - 1, 2)
        )
        value = 0.75 * value + 0.25 * other
        other = jnp.where(
            level % 2 == 0, pltpu.roll(value, 1, 1), pltpu.roll(value, CZ - 1, 1)
        )
        other = jnp.where((level == 0) | (level == CZ - 1), 0.0, other)
        masked[pl.ds(row, chunk)] = 0.75 * value + 0.25 * other

    rows_loop(5, 25, 2, spread)

    def correct(row, chunk=2):
        for i in range(chunk):
            here = 0.75 * masked[row + i]
            for fine, side in (
                (2 * (row + i), masked[row + i - 1]),
                (2 * (row + i) + 1, masked[row + i + 1]),
            ):
                water = wet[fine]
                value = state[fine] + water * (here + 0.25 * side)
                state[fine] = value
                flow[fine] = water * value

    rows_loop(5, 25, 2, correct)

    def smooth_third(row, chunk=4):
        rows = pl.ds(row, chunk)
        value = 0.2 * state[rows] + base[rows] + gain[rows] * near_rows(flow, row, chunk, 1)
        state[rows] = value
        flow_next[rows] = wet[rows] * value

    rows_loop(12, 48, 4, smooth_third)

    def smooth_fourth(row, chunk=2):
        rows = pl.ds(row, chunk)
        value = 0.2 * state[rows] + base[rows] + gain[rows] * near_rows(flow_next, row, chunk, 1)
        state[rows] = value
        flow[rows] = wet[rows] * value

    rows_loop(13, 47, 2, smooth_fourth)

    def finish(row, chunk=4):
        rows = pl.ds(row, chunk)
        value = state[rows]
        left_over = rhs[rows] - diag[rows] * value + wet[rows] * near_rows(flow, row, chunk, 1)
        for i in range(chunk):
            place = pl.ds(row - RIM + i, CZ, stride=ROWS)
            pressure_ref[place, :] = value[i, :, :LANES]
            residual_ref[place, :] = left_over[i, :, :LANES]

    rows_loop(RIM, RIM + ROWS, 4, finish)


def shifted(array, axis, step):
    devices = lax.axis_size(axis)
    pairs = [(i, i + step) for i in range(devices) if 0 <= i + step < devices]
    return lax.ppermute(array, axis, pairs)


def f32(*shape):
    return jax.ShapeDtypeStruct(shape, jnp.float32)


def body(right_side, wet_mask, helmholtz, eig_low, eig_high):
    flat = (CZ * ROWS, LANES)
    right_flat = right_side.reshape(flat)
    mask_flat = wet_mask.reshape(flat)
    helm_flat = helmholtz.reshape(flat)
    limits = pltpu.CompilerParams(vmem_limit_bytes=16 * 1024 * 1024)

    first, last = pl.pallas_call(
        strips_kernel,
        out_shape=(f32(STRIP, CZ, LANES),) * 2,
        in_specs=[VMEM] * 3,
        out_specs=(VMEM,) * 2,
        compiler_params=limits,
        name="strips",
    )(right_flat, mask_flat, helm_flat)
    before = shifted(last, "wide", 1)
    after = shifted(first, "wide", -1)

    tall, first, last = pl.pallas_call(
        sides_kernel,
        out_shape=(
            f32(3, TALL, CZ, LANES),
            f32(3 * PACKED, CZ, LANES),
            f32(3 * PACKED, CZ, LANES),
        ),
        in_specs=[VMEM] * 5,
        out_specs=(VMEM,) * 3,
        compiler_params=limits,
        name="sides",
    )(right_flat, mask_flat, helm_flat, before, after)
    from_left = shifted(last, "narrow", 1)
    from_right = shifted(first, "narrow", -1)

    pressure, residual = pl.pallas_call(
        cycle_kernel,
        out_shape=(f32(*flat),) * 2,
        in_specs=[SMEM] * 2 + [VMEM] * 3,
        out_specs=(VMEM,) * 2,
        scratch_shapes=[pltpu.VMEM((TALL, CZ, WIDE), jnp.float32)] * 9
        + [pltpu.VMEM((TALL // 2, CZ, WIDE), jnp.float32)] * 8,
        compiler_params=limits,
        name="cycle",
    )(eig_low, eig_high, tall, from_left, from_right)
    shape = (CZ, ROWS, LANES)
    return pressure.reshape(shape), residual.reshape(shape)


def solution(mesh):
    field = P(None, "wide", "narrow")
    return jax.shard_map(
        body,
        mesh=mesh,
        in_specs=(field, field, field, P(), P()),
        out_specs=(field, field),
        check_vma=False,
    )
```

```python
import functools

import jax
import jax.numpy as jnp
from jax import lax
from jax.experimental import pallas as pl
from jax.experimental.pallas import tpu as pltpu
from jax.sharding import PartitionSpec as P

CHEB = 4

CZ = 8
ROWS = 32
LANES = 128
RIM = 14
TALL = ROWS + 2 * RIM
MASK_RIM = 13
RIGHT_RIM = 12
STRIP = MASK_RIM + 2 * RIGHT_RIM
SIDE = 16
GROUP = LANES // SIDE
PACKED = 8
PITCH = 2 * CZ

VMEM = pl.BlockSpec(memory_space=pltpu.VMEM)
ANY = pl.BlockSpec(memory_space=pl.ANY)
SMEM = pl.BlockSpec(memory_space=pltpu.SMEM)


def brick_row(ref, row):
    return ref[pl.ds(row, CZ, stride=ROWS), :]


def strips_kernel(right_ref, mask_ref, helm_ref, first_ref, last_ref):
    for out_ref, mask_from, other_from in (
        (first_ref, 0, 0),
        (last_ref, ROWS - MASK_RIM, ROWS - RIGHT_RIM),
    ):
        for row in range(MASK_RIM):
            out_ref[row] = brick_row(mask_ref, mask_from + row).astype(jnp.float32)
        for row in range(RIGHT_RIM):
            out_ref[MASK_RIM + row] = brick_row(helm_ref, other_from + row)
            out_ref[MASK_RIM + RIGHT_RIM + row] = brick_row(right_ref, other_from + row)


def sides_kernel(
    right_ref, mask_ref, helm_ref, before_ref, after_ref, tall_ref, first_ref, last_ref
):
    zero = jnp.zeros((CZ, LANES), jnp.float32)
    for field in range(3):
        for row in (0, 1, TALL - 2, TALL - 1):
            tall_ref[field, row] = zero
    for field, own_ref, offset, rim in (
        (0, mask_ref, 0, MASK_RIM),
        (1, helm_ref, MASK_RIM, RIGHT_RIM),
        (2, right_ref, MASK_RIM + RIGHT_RIM, RIGHT_RIM),
    ):
        for row in range(rim):
            tall_ref[field, RIM - rim + row] = before_ref[offset + row]
            tall_ref[field, RIM + ROWS + row] = after_ref[offset + row]
        for row in range(ROWS):
            tall_ref[field, RIM + row] = brick_row(own_ref, row).astype(jnp.float32)
    lane = lax.broadcasted_iota(jnp.int32, (CZ, LANES), 1)
    for field in range(3):

        def pack(group, carry):
            first, last = zero, zero
            for k in range(GROUP):
                line = tall_ref[field, jnp.minimum(group * GROUP + k, TALL - 1)]
                here = (lane >= SIDE * k) & (lane < SIDE * (k + 1))
                one = pltpu.roll(line, SIDE * k, 1) if k else line
                two = pltpu.roll(line, (SIDE * (k + 1)) % LANES, 1) if k + 1 < GROUP else line
                first = jnp.where(here, one, first)
                last = jnp.where(here, two, last)
            first_ref[field * PACKED + group] = first
            last_ref[field * PACKED + group] = last
            return carry

        lax.fori_loop(0, PACKED, pack, 0)


def rows_loop(start, stop, chunk, step):
    count = (stop - start) // chunk
    assert count * chunk == stop - start

    def body(index, carry):
        step(start + index * chunk, chunk)
        return carry

    lax.fori_loop(0, count, body, 0)


def cycle_kernel(
    eig_low_ref,
    eig_high_ref,
    tall_ref,
    left_ref,
    right_ref,
    pressure_out,
    residual_out,
    wet,
    flow,
    flow_next,
    helm,
    rhs,
    diag,
    base,
    gain,
    state,
    wet_c,
    masked,
    masked_next,
    diag_c,
    inverse_c,
    remain,
    error,
    direction,
    pressure_ref,
    residual_ref,
    out_sem,
):
    lane = lax.broadcasted_iota(jnp.int32, (CZ, LANES), 1)
    level = lax.broadcasted_iota(jnp.int32, (CZ, LANES), 0)
    zero = jnp.zeros((CZ, LANES), jnp.float32)
    tiles = (0, 1)

    def put(ref, tile, row, value):
        ref[tile, pl.ds(row * PITCH + CZ, CZ), :] = value

    def get(ref, tile, row, shift=0):
        return ref[tile, pl.ds(row * PITCH + (CZ + shift), CZ), :]

    def clear(ref, first, last):
        def body(row, carry):
            for tile in tiles:
                ref[tile, pl.ds(row * PITCH, CZ), :] = zero
            return carry

        lax.fori_loop(first, last + 1, body, 0, unroll=8)

    for ref in (wet, flow, flow_next):
        clear(ref, 0, TALL)
    for ref in (wet_c, masked, masked_next):
        clear(ref, 0, TALL // 2)

    def beside(main, side, reach):
        low, high = lane < reach, lane >= LANES - reach
        main_up, side_up = pltpu.roll(main, reach, 1), pltpu.roll(side, reach, 1)
        main_down = pltpu.roll(main, LANES - reach, 1)
        side_down = pltpu.roll(side, LANES - reach, 1)
        return (
            (jnp.where(low, side_up, main_up), jnp.where(high, side_down, main_down)),
            (jnp.where(low, main_up, side_up), jnp.where(high, main_down, side_down)),
        )

    def near_rows(ref, row, count, reach):
        lines = [[get(ref, tile, row + k - 1) for tile in tiles] for k in range(2)]
        for k in range(count):
            lines.append([get(ref, tile, row + k + 1) for tile in tiles])
            here = lines[k + 1]
            sides = beside(here[0], here[1], reach)
            yield [
                (lines[k][tile] + lines[k + 2][tile])
                + (get(ref, tile, row + k, -reach) + get(ref, tile, row + k, reach))
                + (sides[tile][0] + sides[tile][1])
                for tile in tiles
            ]

    def unpack(first_group, groups):
        for i in range(groups):
            group = first_group + i
            for field in range(3):
                after = right_ref[field * PACKED + group]
                ahead = pltpu.roll(left_ref[field * PACKED + group], LANES - SIDE, 1)
                for k in range(GROUP):
                    row = jnp.minimum(group * GROUP + k, TALL - 1)
                    low, high = SIDE * k, SIDE * (k + 1)
                    beyond = (low - SIDE) % LANES
                    both = jnp.where((lane >= beyond) & (lane < beyond + SIDE), ahead, 0.0)
                    both = jnp.where((lane >= low) & (lane < high), after, both)
                    if k:
                        both = pltpu.roll(both, LANES - low, 1)
                    main = tall_ref[field, row]
                    if field == 0:
                        put(wet, 0, row, main)
                        put(wet, 1, row, both)
                    else:
                        dest = (helm, rhs)[field - 1]
                        dest[0, row] = main
                        dest[1, row] = both

    rows_loop(0, PACKED, 2, unpack)

    def smooth_setup(row, chunk):
        for k, count in enumerate(near_rows(wet, row, chunk, 1)):
            for tile in tiles:
                water = get(wet, tile, row + k)
                scale = water * (helm[tile, row + k] + count[tile]) + (1.0 - water)
                inverse = 0.8 / scale
                start = inverse * rhs[tile, row + k]
                diag[tile, row + k] = scale
                base[tile, row + k] = start
                gain[tile, row + k] = inverse * water
                put(flow, tile, row + k, water * start)

    rows_loop(2, 58, 14, smooth_setup)

    def smooth_second(row, chunk):
        for k, near in enumerate(near_rows(flow, row, chunk, 1)):
            for tile in tiles:
                value = 1.2 * base[tile, row + k] + gain[tile, row + k] * near[tile]
                state[tile, row + k] = value
                put(flow_next, tile, row + k, get(wet, tile, row + k) * value)

    rows_loop(3, 57, 18, smooth_second)

    def pair_sum(value):
        value = value + jnp.where(
            level % 2 == 0, pltpu.roll(value, CZ - 1, 0), pltpu.roll(value, 1, 0)
        )
        return value + jnp.where(
            lane % 2 == 0, pltpu.roll(value, LANES - 1, 1), pltpu.roll(value, 1, 1)
        )

    def coarse_mask(row, chunk):
        for k in range(chunk):
            for tile in tiles:
                fine = 2 * (row + k)
                total = pair_sum(get(wet, tile, fine) + get(wet, tile, fine + 1))
                put(wet_c, tile, row + k, jnp.where(total >= 3.5, 1.0, 0.0))

    rows_loop(1, 29, 14, coarse_mask)

    low = jnp.full((CZ, LANES), eig_low_ref[0], jnp.float32)
    high = jnp.full((CZ, LANES), eig_high_ref[0], jnp.float32)
    centre = 0.5 * (high + low)
    half = 0.5 * (high - low)
    sigma = centre / half
    rho = 1.0 / sigma
    start_scale = 1.0 / centre

    def coarse_setup(row, chunk):
        fine_near = near_rows(flow_next, 2 * row, 2 * chunk, 1)
        for k, count_c in enumerate(near_rows(wet_c, row, chunk, 2)):
            source, shift = [zero, zero], [zero, zero]
            for fine in (2 * (row + k), 2 * (row + k) + 1):
                near = next(fine_near)
                for tile in tiles:
                    left_over = rhs[tile, fine] - diag[tile, fine] * state[tile, fine]
                    source[tile] += get(wet, tile, fine) * (left_over + near[tile])
                    shift[tile] += helm[tile, fine]
            for tile in tiles:
                first_sum = 0.125 * pair_sum(source[tile])
                water_c = get(wet_c, tile, row + k)
                scale = water_c * (0.125 * pair_sum(shift[tile]) + 0.25 * count_c[tile])
                scale = scale + (1.0 - water_c)
                inverse = 1.0 / scale
                first = first_sum * inverse * start_scale
                diag_c[tile, row + k] = scale
                inverse_c[tile, row + k] = inverse
                remain[tile, row + k] = first_sum
                error[tile, row + k] = first
                direction[tile, row + k] = first
                put(masked, tile, row + k, water_c * first)

    rows_loop(2, 28, 13, coarse_setup)

    now, later = masked, masked_next
    for sweep in range(1, CHEB):
        rho_next = 1.0 / (2.0 * sigma - rho)
        keep = rho_next * rho
        add = 2.0 * rho_next / half

        def chebyshev(row, chunk, keep=keep, add=add, now=now, later=later):
            for k, near in enumerate(near_rows(now, row, chunk, 2)):
                for tile in tiles:
                    old = direction[tile, row + k]
                    water_c = get(wet_c, tile, row + k)
                    image = diag_c[tile, row + k] * old - 0.25 * water_c * near[tile]
                    left_over = remain[tile, row + k] - image
                    fresh = keep * old + add * (left_over * inverse_c[tile, row + k])
                    remain[tile, row + k] = left_over
                    direction[tile, row + k] = fresh
                    error[tile, row + k] = error[tile, row + k] + fresh
                    put(later, tile, row + k, water_c * fresh)

        rows_loop(2 + sweep, 28 - sweep, 13 - sweep, chebyshev)
        rho = rho_next
        now, later = later, now

    def spread(row, chunk):
        for k in range(chunk):
            value = [error[tile, row + k] for tile in tiles]
            sides = beside(value[0], value[1], 1)
            for tile in tiles:
                line = 0.75 * value[tile] + 0.25 * jnp.where(
                    lane % 2 == 0, sides[tile][0], sides[tile][1]
                )
                other = jnp.where(level % 2 == 0, pltpu.roll(line, 1, 0), pltpu.roll(line, CZ - 1, 0))
                other = jnp.where((level == 0) | (level == CZ - 1), 0.0, other)
                direction[tile, row + k] = 0.75 * line + 0.25 * other

    rows_loop(5, 25, 10, spread)

    def correct(row, chunk):
        for k in range(chunk):
            for tile in tiles:
                here = 0.75 * direction[tile, row + k]
                for fine, side in ((2 * (row + k), row + k - 1), (2 * (row + k) + 1, row + k + 1)):
                    water = get(wet, tile, fine)
                    value = state[tile, fine] + water * (here + 0.25 * direction[tile, side])
                    state[tile, fine] = value
                    put(flow, tile, fine, water * value)

    rows_loop(5, 25, 10, correct)

    def smooth(now, later):
        def step(row, chunk):
            for k, near in enumerate(near_rows(now, row, chunk, 1)):
                for tile in tiles:
                    value = 0.2 * state[tile, row + k] + base[tile, row + k]
                    value = value + gain[tile, row + k] * near[tile]
                    state[tile, row + k] = value
                    put(later, tile, row + k, get(wet, tile, row + k) * value)

        return step

    rows_loop(12, 48, 12, smooth(flow, flow_next))
    rows_loop(13, 47, 17, smooth(flow_next, flow))

    def finish_pressure(row, chunk):
        for k in range(chunk):
            pressure_ref[pl.ds(row + k - RIM, CZ, stride=ROWS), :] = state[0, row + k]

    rows_loop(RIM, RIM + ROWS, 16, finish_pressure)
    pressure_copy = pltpu.make_async_copy(pressure_ref, pressure_out, out_sem.at[0])
    pressure_copy.start()

    def finish(row, chunk):
        for k, near in enumerate(near_rows(flow, row, chunk, 1)):
            left_over = rhs[0, row + k] - diag[0, row + k] * state[0, row + k]
            left_over = left_over + get(wet, 0, row + k) * near[0]
            residual_ref[pl.ds(row + k - RIM, CZ, stride=ROWS), :] = left_over

    rows_loop(RIM, RIM + ROWS, 16, finish)
    residual_copy = pltpu.make_async_copy(residual_ref, residual_out, out_sem.at[1])
    residual_copy.start()
    pressure_copy.wait()
    residual_copy.wait()


def shifted(array, axis, step):
    devices = lax.axis_size(axis)
    pairs = [(i, i + step) for i in range(devices) if 0 <= i + step < devices]
    return lax.ppermute(array, axis, pairs)


def f32(*shape):
    return jax.ShapeDtypeStruct(shape, jnp.float32)


def body(right_side, wet_mask, helmholtz, eig_low, eig_high):
    flat = (CZ * ROWS, LANES)
    right_flat = right_side.reshape(flat)
    mask_flat = wet_mask.reshape(flat)
    helm_flat = helmholtz.reshape(flat)
    limits = pltpu.CompilerParams(vmem_limit_bytes=24 * 1024 * 1024)

    first, last = pl.pallas_call(
        strips_kernel,
        out_shape=(f32(STRIP, CZ, LANES),) * 2,
        in_specs=[VMEM] * 3,
        out_specs=(VMEM,) * 2,
        compiler_params=limits,
        name="strips",
    )(right_flat, mask_flat, helm_flat)
    before = shifted(last, "wide", 1)
    after = shifted(first, "wide", -1)

    tall, first, last = pl.pallas_call(
        sides_kernel,
        out_shape=(
            f32(3, TALL, CZ, LANES),
            f32(3 * PACKED, CZ, LANES),
            f32(3 * PACKED, CZ, LANES),
        ),
        in_specs=[VMEM] * 5,
        out_specs=(VMEM,) * 3,
        compiler_params=limits,
        name="sides",
    )(right_flat, mask_flat, helm_flat, before, after)
    from_left = shifted(last, "narrow", 1)
    from_right = shifted(first, "narrow", -1)

    pressure, residual = pl.pallas_call(
        cycle_kernel,
        out_shape=(f32(*flat),) * 2,
        in_specs=[SMEM] * 2 + [VMEM] * 3,
        out_specs=(ANY,) * 2,
        scratch_shapes=[pltpu.VMEM((2, TALL * PITCH + CZ, LANES), jnp.float32)] * 3
        + [pltpu.VMEM((2, TALL, CZ, LANES), jnp.float32)] * 6
        + [pltpu.VMEM((2, TALL // 2 * PITCH + CZ, LANES), jnp.float32)] * 3
        + [pltpu.VMEM((2, TALL // 2, CZ, LANES), jnp.float32)] * 5
        + [pltpu.VMEM(flat, jnp.float32)] * 2
        + [pltpu.SemaphoreType.DMA((2,))],
        compiler_params=limits,
        name="cycle",
    )(eig_low, eig_high, tall, from_left, from_right)
    shape = (CZ, ROWS, LANES)
    return pressure.reshape(shape), residual.reshape(shape)


def solution(mesh):
    field = P(None, "wide", "narrow")
    return jax.shard_map(
        body,
        mesh=mesh,
        in_specs=(field, field, field, P(), P()),
        out_specs=(field, field),
        check_vma=False,
    )
```

```python
import functools

import jax
import jax.numpy as jnp
from jax import lax
from jax.experimental import pallas as pl
from jax.experimental.pallas import tpu as pltpu
from jax.sharding import PartitionSpec as P

CHEB = 4

CZ = 8
ROWS = 32
LANES = 128
RIM = 14
TALL = ROWS + 2 * RIM
MASK_RIM = 13
RIGHT_RIM = 12
STRIP = MASK_RIM + 2 * RIGHT_RIM
SIDE = 16
GROUP = LANES // SIDE
PACKED = 8
PITCH = 2 * CZ

VMEM = pl.BlockSpec(memory_space=pltpu.VMEM)
SMEM = pl.BlockSpec(memory_space=pltpu.SMEM)
HBM = pl.BlockSpec(memory_space=pltpu.HBM)


def brick_row(ref, row):
    return ref[pl.ds(row, CZ, stride=ROWS), :]


def strips_kernel(
    right_hbm, mask_hbm, helm_hbm, first_ref, last_ref, own_ref, mask_ref, helm_ref, right_ref, sem
):
    copies = [
        pltpu.make_async_copy(source, dest, sem.at[k])
        for k, (source, dest) in enumerate(
            ((mask_hbm, mask_ref), (helm_hbm, helm_ref), (right_hbm, right_ref))
        )
    ]
    for copy in copies:
        copy.start()
    for field, (ref, rim, offset) in enumerate(
        (
            (mask_ref, MASK_RIM, 0),
            (helm_ref, RIGHT_RIM, MASK_RIM),
            (right_ref, RIGHT_RIM, MASK_RIM + RIGHT_RIM),
        )
    ):
        copies[field].wait()
        for row in range(ROWS):
            line = brick_row(ref, row).astype(jnp.float32)
            own_ref[field, row] = line
            if row < rim:
                first_ref[offset + row] = line
            if row >= ROWS - rim:
                last_ref[offset + row - (ROWS - rim)] = line


def sides_kernel(
    low_ref, high_ref, own_ref, before_ref, after_ref, tall_ref, first_ref, last_ref, eig_ref
):
    eig_ref[0] = jnp.full((CZ, LANES), low_ref[0], jnp.float32)
    eig_ref[1] = jnp.full((CZ, LANES), high_ref[0], jnp.float32)
    zero = jnp.zeros((CZ, LANES), jnp.float32)
    lane = lax.broadcasted_iota(jnp.int32, (CZ, LANES), 1)
    for field, offset, rim in (
        (0, 0, MASK_RIM),
        (1, MASK_RIM, RIGHT_RIM),
        (2, MASK_RIM + RIGHT_RIM, RIGHT_RIM),
    ):
        for row in (0, 1, TALL - 2, TALL - 1):
            tall_ref[field, row] = zero
        for row in range(rim):
            tall_ref[field, RIM - rim + row] = before_ref[offset + row]
            tall_ref[field, RIM + ROWS + row] = after_ref[offset + row]
        for row in range(ROWS):
            tall_ref[field, RIM + row] = own_ref[field, row]

    def pack(first_group, groups):
        for i in range(groups):
            group = first_group + i
            for field in range(3):
                first, last = [], []
                for k in range(GROUP):
                    line = tall_ref[field, jnp.minimum(group * GROUP + k, TALL - 1)]
                    here = (lane >= SIDE * k) & (lane < SIDE * (k + 1))
                    one = pltpu.roll(line, SIDE * k, 1) if k else line
                    two = pltpu.roll(line, SIDE * (k + 1), 1) if k + 1 < GROUP else line
                    first.append(jnp.where(here, one, 0.0))
                    last.append(jnp.where(here, two, 0.0))
                for ref, parts in ((first_ref, first), (last_ref, last)):
                    while len(parts) > 1:
                        parts = [x + y for x, y in zip(parts[::2], parts[1::2])]
                    ref[field * PACKED + group] = parts[0]

    rows_loop(0, PACKED, 2, pack)


def rows_loop(start, stop, chunk, step):
    count = (stop - start) // chunk
    assert count * chunk == stop - start

    def body(index, carry):
        step(start + index * chunk, chunk)
        return carry

    lax.fori_loop(0, count, body, 0)


def cycle_kernel(
    eig_ref,
    tall_ref,
    left_ref,
    right_ref,
    pressure_out,
    residual_out,
    wet,
    flow,
    flow_next,
    helm,
    rhs,
    diag,
    base,
    gain,
    state,
    wet_c,
    masked,
    masked_next,
    diag_c,
    inverse_c,
    remain,
    error,
    direction,
    pressure_ref,
    residual_ref,
    out_sem,
):
    lane = lax.broadcasted_iota(jnp.int32, (CZ, LANES), 1)
    level = lax.broadcasted_iota(jnp.int32, (CZ, LANES), 0)
    zero = jnp.zeros((CZ, LANES), jnp.float32)
    tiles = (0, 1)

    def put(ref, tile, row, value):
        ref[tile, pl.ds(row * PITCH + CZ, CZ), :] = value

    def get(ref, tile, row, shift=0):
        return ref[tile, pl.ds(row * PITCH + (CZ + shift), CZ), :]

    def clear(ref, first, last):
        def body(row, carry):
            for tile in tiles:
                ref[tile, pl.ds(row * PITCH, CZ), :] = zero
            return carry

        lax.fori_loop(first, last + 1, body, 0, unroll=8)

    for ref in (wet, flow, flow_next):
        clear(ref, 0, TALL)
    for ref in (wet_c, masked, masked_next):
        clear(ref, 0, TALL // 2)

    def beside(main, side, reach):
        low, high = lane < reach, lane >= LANES - reach
        main_up, side_up = pltpu.roll(main, reach, 1), pltpu.roll(side, reach, 1)
        main_down = pltpu.roll(main, LANES - reach, 1)
        side_down = pltpu.roll(side, LANES - reach, 1)
        return (
            (jnp.where(low, side_up, main_up), jnp.where(high, side_down, main_down)),
            (jnp.where(low, main_up, side_up), jnp.where(high, main_down, side_down)),
        )

    def near_rows(ref, row, count, reach):
        lines = [[get(ref, tile, row + k - 1) for tile in tiles] for k in range(2)]
        for k in range(count):
            lines.append([get(ref, tile, row + k + 1) for tile in tiles])
            here = lines[k + 1]
            sides = beside(here[0], here[1], reach)
            yield [
                (lines[k][tile] + lines[k + 2][tile])
                + (get(ref, tile, row + k, -reach) + get(ref, tile, row + k, reach))
                + (sides[tile][0] + sides[tile][1])
                for tile in tiles
            ]

    def unpack(first_group, groups):
        for i in range(groups):
            group = first_group + i
            for field in range(3):
                after = right_ref[field * PACKED + group]
                ahead = pltpu.roll(left_ref[field * PACKED + group], LANES - SIDE, 1)
                for k in range(GROUP):
                    row = jnp.minimum(group * GROUP + k, TALL - 1)
                    low, high = SIDE * k, SIDE * (k + 1)
                    beyond = (low - SIDE) % LANES
                    both = jnp.where((lane >= beyond) & (lane < beyond + SIDE), ahead, 0.0)
                    both = jnp.where((lane >= low) & (lane < high), after, both)
                    if k:
                        both = pltpu.roll(both, LANES - low, 1)
                    main = tall_ref[field, row]
                    if field == 0:
                        put(wet, 0, row, main)
                        put(wet, 1, row, both)
                    else:
                        dest = (helm, rhs)[field - 1]
                        dest[0, row] = main
                        dest[1, row] = both

    rows_loop(0, PACKED, 2, unpack)

    def smooth_setup(row, chunk):
        for k, count in enumerate(near_rows(wet, row, chunk, 1)):
            for tile in tiles:
                water = get(wet, tile, row + k)
                scale = water * (helm[tile, row + k] + count[tile]) + (1.0 - water)
                inverse = 0.8 / scale
                start = inverse * rhs[tile, row + k]
                diag[tile, row + k] = scale
                base[tile, row + k] = start
                gain[tile, row + k] = inverse * water
                put(flow, tile, row + k, water * start)

    rows_loop(2, 58, 14, smooth_setup)

    def smooth_second(row, chunk):
        for k, near in enumerate(near_rows(flow, row, chunk, 1)):
            for tile in tiles:
                value = 1.2 * base[tile, row + k] + gain[tile, row + k] * near[tile]
                state[tile, row + k] = value
                put(flow_next, tile, row + k, get(wet, tile, row + k) * value)

    rows_loop(3, 57, 18, smooth_second)

    def pair_sum(value):
        value = value + jnp.where(
            level % 2 == 0, pltpu.roll(value, CZ - 1, 0), pltpu.roll(value, 1, 0)
        )
        return value + jnp.where(
            lane % 2 == 0, pltpu.roll(value, LANES - 1, 1), pltpu.roll(value, 1, 1)
        )

    def coarse_mask(row, chunk):
        for k in range(chunk):
            for tile in tiles:
                fine = 2 * (row + k)
                total = pair_sum(get(wet, tile, fine) + get(wet, tile, fine + 1))
                put(wet_c, tile, row + k, jnp.where(total >= 3.5, 1.0, 0.0))

    rows_loop(1, 29, 14, coarse_mask)

    low, high = eig_ref[0], eig_ref[1]
    centre = 0.5 * (high + low)
    half = 0.5 * (high - low)
    sigma = centre / half
    rho = 1.0 / sigma
    start_scale = 1.0 / centre

    def coarse_setup(row, chunk):
        fine_near = near_rows(flow_next, 2 * row, 2 * chunk, 1)
        for k, count_c in enumerate(near_rows(wet_c, row, chunk, 2)):
            source, shift = [zero, zero], [zero, zero]
            for fine in (2 * (row + k), 2 * (row + k) + 1):
                near = next(fine_near)
                for tile in tiles:
                    left_over = rhs[tile, fine] - diag[tile, fine] * state[tile, fine]
                    source[tile] += get(wet, tile, fine) * (left_over + near[tile])
                    shift[tile] += helm[tile, fine]
            for tile in tiles:
                first_sum = 0.125 * pair_sum(source[tile])
                water_c = get(wet_c, tile, row + k)
                scale = water_c * (0.125 * pair_sum(shift[tile]) + 0.25 * count_c[tile])
                scale = scale + (1.0 - water_c)
                inverse = 1.0 / scale
                first = first_sum * inverse * start_scale
                diag_c[tile, row + k] = scale
                inverse_c[tile, row + k] = inverse
                remain[tile, row + k] = first_sum
                error[tile, row + k] = first
                direction[tile, row + k] = first
                put(masked, tile, row + k, water_c * first)

    rows_loop(2, 28, 13, coarse_setup)

    now, later = masked, masked_next
    for sweep in range(1, CHEB):
        rho_next = 1.0 / (2.0 * sigma - rho)
        keep = rho_next * rho
        add = 2.0 * rho_next / half

        def chebyshev(row, chunk, keep=keep, add=add, now=now, later=later):
            for k, near in enumerate(near_rows(now, row, chunk, 2)):
                for tile in tiles:
                    old = direction[tile, row + k]
                    water_c = get(wet_c, tile, row + k)
                    image = diag_c[tile, row + k] * old - 0.25 * water_c * near[tile]
                    left_over = remain[tile, row + k] - image
                    fresh = keep * old + add * (left_over * inverse_c[tile, row + k])
                    remain[tile, row + k] = left_over
                    direction[tile, row + k] = fresh
                    error[tile, row + k] = error[tile, row + k] + fresh
                    put(later, tile, row + k, water_c * fresh)

        rows_loop(2 + sweep, 28 - sweep, 13 - sweep, chebyshev)
        rho = rho_next
        now, later = later, now

    def spread(row, chunk):
        for k in range(chunk):
            value = [error[tile, row + k] for tile in tiles]
            sides = beside(value[0], value[1], 1)
            for tile in tiles:
                line = 0.75 * value[tile] + 0.25 * jnp.where(
                    lane % 2 == 0, sides[tile][0], sides[tile][1]
                )
                other = jnp.where(level % 2 == 0, pltpu.roll(line, 1, 0), pltpu.roll(line, CZ - 1, 0))
                other = jnp.where((level == 0) | (level == CZ - 1), 0.0, other)
                direction[tile, row + k] = 0.75 * line + 0.25 * other

    rows_loop(5, 25, 10, spread)

    def correct(row, chunk):
        for k in range(chunk):
            for tile in tiles:
                here = 0.75 * direction[tile, row + k]
                for fine, side in ((2 * (row + k), row + k - 1), (2 * (row + k) + 1, row + k + 1)):
                    water = get(wet, tile, fine)
                    value = state[tile, fine] + water * (here + 0.25 * direction[tile, side])
                    state[tile, fine] = value
                    put(flow, tile, fine, water * value)

    rows_loop(5, 25, 10, correct)

    def smooth(now, later):
        def step(row, chunk):
            for k, near in enumerate(near_rows(now, row, chunk, 1)):
                for tile in tiles:
                    value = 0.2 * state[tile, row + k] + base[tile, row + k]
                    value = value + gain[tile, row + k] * near[tile]
                    state[tile, row + k] = value
                    put(later, tile, row + k, get(wet, tile, row + k) * value)

        return step

    rows_loop(12, 48, 12, smooth(flow, flow_next))
    rows_loop(13, 47, 17, smooth(flow_next, flow))

    def finish_pressure(row, chunk):
        for k in range(chunk):
            pressure_ref[pl.ds(row + k - RIM, CZ, stride=ROWS), :] = state[0, row + k]

    rows_loop(RIM, RIM + ROWS, 16, finish_pressure)
    pressure_copy = pltpu.make_async_copy(pressure_ref, pressure_out, out_sem.at[0])
    pressure_copy.start()

    def finish(row, chunk):
        for k, near in enumerate(near_rows(flow, row, chunk, 1)):
            left_over = rhs[0, row + k] - diag[0, row + k] * state[0, row + k]
            left_over = left_over + get(wet, 0, row + k) * near[0]
            residual_ref[pl.ds(row + k - RIM, CZ, stride=ROWS), :] = left_over

    rows_loop(RIM, RIM + ROWS, 16, finish)
    residual_copy = pltpu.make_async_copy(residual_ref, residual_out, out_sem.at[1])
    residual_copy.start()
    pressure_copy.wait()
    residual_copy.wait()


def shifted(array, axis, step):
    devices = lax.axis_size(axis)
    pairs = [(i, i + step) for i in range(devices) if 0 <= i + step < devices]
    return lax.ppermute(array, axis, pairs)


def in_hbm(array):
    return pltpu.with_memory_space_constraint(array, pltpu.HBM)


def f32(*shape):
    return jax.ShapeDtypeStruct(shape, jnp.float32)


def body(right_side, wet_mask, helmholtz, eig_low, eig_high):
    flat = (CZ * ROWS, LANES)
    right_flat = right_side.reshape(flat)
    mask_flat = wet_mask.reshape(flat)
    helm_flat = helmholtz.reshape(flat)
    limits = pltpu.CompilerParams(vmem_limit_bytes=24 * 1024 * 1024)

    first, last, own = pl.pallas_call(
        strips_kernel,
        out_shape=(f32(STRIP, CZ, LANES), f32(STRIP, CZ, LANES), f32(3, ROWS, CZ, LANES)),
        in_specs=[HBM] * 3,
        out_specs=(VMEM,) * 3,
        scratch_shapes=[
            pltpu.VMEM(flat, jnp.int32),
            pltpu.VMEM(flat, jnp.float32),
            pltpu.VMEM(flat, jnp.float32),
            pltpu.SemaphoreType.DMA((3,)),
        ],
        compiler_params=limits,
        name="strips",
    )(in_hbm(right_flat), in_hbm(mask_flat), in_hbm(helm_flat))
    before = shifted(last, "wide", 1)
    after = shifted(first, "wide", -1)

    tall, first, last, eigs = pl.pallas_call(
        sides_kernel,
        out_shape=(
            f32(3, TALL, CZ, LANES),
            f32(3 * PACKED, CZ, LANES),
            f32(3 * PACKED, CZ, LANES),
            f32(2, CZ, LANES),
        ),
        in_specs=[SMEM] * 2 + [VMEM] * 3,
        out_specs=(VMEM,) * 4,
        compiler_params=limits,
        name="sides",
    )(eig_low, eig_high, own, before, after)
    from_left = shifted(last, "narrow", 1)
    from_right = shifted(first, "narrow", -1)

    pressure, residual = pl.pallas_call(
        cycle_kernel,
        out_shape=(f32(*flat),) * 2,
        in_specs=[VMEM] * 4,
        out_specs=(HBM,) * 2,
        scratch_shapes=[pltpu.VMEM((2, TALL * PITCH + CZ, LANES), jnp.float32)] * 3
        + [pltpu.VMEM((2, TALL, CZ, LANES), jnp.float32)] * 6
        + [pltpu.VMEM((2, TALL // 2 * PITCH + CZ, LANES), jnp.float32)] * 3
        + [pltpu.VMEM((2, TALL // 2, CZ, LANES), jnp.float32)] * 5
        + [pltpu.VMEM(flat, jnp.float32)] * 2
        + [pltpu.SemaphoreType.DMA((2,))],
        compiler_params=limits,
        name="cycle",
    )(eigs, tall, from_left, from_right)
    shape = (CZ, ROWS, LANES)
    return pressure.reshape(shape), residual.reshape(shape)


def solution(mesh):
    field = P(None, "wide", "narrow")
    return jax.shard_map(
        body,
        mesh=mesh,
        in_specs=(field, field, field, P(), P()),
        out_specs=(field, field),
        check_vma=False,
    )
```

```python
import functools

import jax
import jax.numpy as jnp
from jax import lax
from jax.experimental import pallas as pl
from jax.experimental.pallas import tpu as pltpu
from jax.sharding import PartitionSpec as P

CHEB = 4

CZ = 8
ROWS = 32
LANES = 128
RIM = 14
TALL = ROWS + 2 * RIM
MASK_RIM = 13
RIGHT_RIM = 12
STRIP = MASK_RIM + 2 * RIGHT_RIM
SIDE = 16
GROUP = LANES // SIDE
PACKED = 8
PITCH = 2 * CZ

VMEM = pl.BlockSpec(memory_space=pltpu.VMEM)
SMEM = pl.BlockSpec(memory_space=pltpu.SMEM)
HBM = pl.BlockSpec(memory_space=pltpu.HBM)


def brick_row(ref, row):
    return ref[pl.ds(row, CZ, stride=ROWS), :]


def strips_kernel(
    right_hbm, mask_hbm, helm_hbm, far_ref, near_ref, own_ref, mask_ref, helm_ref, right_ref, sem
):
    odd = lax.rem(lax.axis_index("wide"), 2)
    copies = [
        pltpu.make_async_copy(source, dest, sem.at[k])
        for k, (source, dest) in enumerate(
            ((mask_hbm, mask_ref), (helm_hbm, helm_ref), (right_hbm, right_ref))
        )
    ]
    for copy in copies:
        copy.start()
    for field, (ref, rim, offset) in enumerate(
        (
            (mask_ref, MASK_RIM, 0),
            (helm_ref, RIGHT_RIM, MASK_RIM),
            (right_ref, RIGHT_RIM, MASK_RIM + RIGHT_RIM),
        )
    ):
        copies[field].wait()
        for row in range(ROWS):
            line = brick_row(ref, row).astype(jnp.float32)
            own_ref[field, row] = line
        to_far, to_near = (ROWS - rim) * odd, (ROWS - rim) * (1 - odd)
        for row in range(rim):
            far_ref[offset + row] = own_ref[field, to_far + row]
            near_ref[offset + row] = own_ref[field, to_near + row]


def sides_kernel(
    low_ref, high_ref, own_ref, far_ref, near_ref, tall_ref, far_out, near_out, eig_ref
):
    odd = lax.rem(lax.axis_index("wide"), 2)
    odd_column = lax.rem(lax.axis_index("narrow"), 2) == 1
    eig_ref[0] = jnp.full((CZ, LANES), low_ref[0], jnp.float32)
    eig_ref[1] = jnp.full((CZ, LANES), high_ref[0], jnp.float32)
    zero = jnp.zeros((CZ, LANES), jnp.float32)
    lane = lax.broadcasted_iota(jnp.int32, (CZ, LANES), 1)
    for field, offset, rim in (
        (0, 0, MASK_RIM),
        (1, MASK_RIM, RIGHT_RIM),
        (2, MASK_RIM + RIGHT_RIM, RIGHT_RIM),
    ):
        for row in (0, 1, TALL - 2, TALL - 1):
            tall_ref[field, row] = zero
        from_far = RIM - rim + (ROWS + rim) * odd
        from_near = RIM - rim + (ROWS + rim) * (1 - odd)
        for row in range(rim):
            tall_ref[field, from_far + row] = far_ref[offset + row]
            tall_ref[field, from_near + row] = near_ref[offset + row]
        for row in range(ROWS):
            tall_ref[field, RIM + row] = own_ref[field, row]

    def pack(first_group, groups):
        for i in range(groups):
            group = first_group + i
            for field in range(3):
                first, last = [], []
                for k in range(GROUP):
                    line = tall_ref[field, jnp.minimum(group * GROUP + k, TALL - 1)]
                    here = (lane >= SIDE * k) & (lane < SIDE * (k + 1))
                    one = pltpu.roll(line, SIDE * k, 1) if k else line
                    two = pltpu.roll(line, SIDE * (k + 1), 1) if k + 1 < GROUP else line
                    first.append(jnp.where(here, one, 0.0))
                    last.append(jnp.where(here, two, 0.0))
                while len(first) > 1:
                    first = [x + y for x, y in zip(first[::2], first[1::2])]
                    last = [x + y for x, y in zip(last[::2], last[1::2])]
                place = field * PACKED + group
                far_out[place] = jnp.where(odd_column, last[0], first[0])
                near_out[place] = jnp.where(odd_column, first[0], last[0])

    rows_loop(0, PACKED, 2, pack)


def rows_loop(start, stop, chunk, step):
    count = (stop - start) // chunk
    assert count * chunk == stop - start

    def body(index, carry):
        step(start + index * chunk, chunk)
        return carry

    lax.fori_loop(0, count, body, 0)


def cycle_kernel(
    eig_ref,
    tall_ref,
    far_ref,
    near_ref,
    pressure_out,
    residual_out,
    wet,
    flow,
    flow_next,
    helm,
    rhs,
    diag,
    base,
    gain,
    state,
    wet_c,
    masked,
    masked_next,
    diag_c,
    inverse_c,
    remain,
    error,
    direction,
    pressure_ref,
    residual_ref,
    out_sem,
):
    lane = lax.broadcasted_iota(jnp.int32, (CZ, LANES), 1)
    level = lax.broadcasted_iota(jnp.int32, (CZ, LANES), 0)
    zero = jnp.zeros((CZ, LANES), jnp.float32)
    tiles = (0, 1)

    def put(ref, tile, row, value):
        ref[tile, pl.ds(row * PITCH + CZ, CZ), :] = value

    def get(ref, tile, row, shift=0):
        return ref[tile, pl.ds(row * PITCH + (CZ + shift), CZ), :]

    def clear(ref, first, last):
        def body(row, carry):
            for tile in tiles:
                ref[tile, pl.ds(row * PITCH, CZ), :] = zero
            return carry

        lax.fori_loop(first, last + 1, body, 0, unroll=8)

    for ref in (wet, flow, flow_next):
        clear(ref, 0, TALL)
    for ref in (wet_c, masked, masked_next):
        clear(ref, 0, TALL // 2)

    def beside(main, side, reach):
        low, high = lane < reach, lane >= LANES - reach
        main_up, side_up = pltpu.roll(main, reach, 1), pltpu.roll(side, reach, 1)
        main_down = pltpu.roll(main, LANES - reach, 1)
        side_down = pltpu.roll(side, LANES - reach, 1)
        return (
            (jnp.where(low, side_up, main_up), jnp.where(high, side_down, main_down)),
            (jnp.where(low, main_up, side_up), jnp.where(high, main_down, side_down)),
        )

    def near_rows(ref, row, count, reach):
        lines = [[get(ref, tile, row + k - 1) for tile in tiles] for k in range(2)]
        for k in range(count):
            lines.append([get(ref, tile, row + k + 1) for tile in tiles])
            here = lines[k + 1]
            sides = beside(here[0], here[1], reach)
            yield [
                (lines[k][tile] + lines[k + 2][tile])
                + (get(ref, tile, row + k, -reach) + get(ref, tile, row + k, reach))
                + (sides[tile][0] + sides[tile][1])
                for tile in tiles
            ]

    odd_column = lax.rem(lax.axis_index("narrow"), 2) == 1

    def unpack(first_group, groups):
        for i in range(groups):
            group = first_group + i
            for field in range(3):
                far, near = far_ref[field * PACKED + group], near_ref[field * PACKED + group]
                after = jnp.where(odd_column, far, near)
                ahead = pltpu.roll(jnp.where(odd_column, near, far), LANES - SIDE, 1)
                for k in range(GROUP):
                    row = jnp.minimum(group * GROUP + k, TALL - 1)
                    low, high = SIDE * k, SIDE * (k + 1)
                    beyond = (low - SIDE) % LANES
                    both = jnp.where((lane >= beyond) & (lane < beyond + SIDE), ahead, 0.0)
                    both = jnp.where((lane >= low) & (lane < high), after, both)
                    if k:
                        both = pltpu.roll(both, LANES - low, 1)
                    main = tall_ref[field, row]
                    if field == 0:
                        put(wet, 0, row, main)
                        put(wet, 1, row, both)
                    else:
                        dest = (helm, rhs)[field - 1]
                        dest[0, row] = main
                        dest[1, row] = both

    rows_loop(0, PACKED, 2, unpack)

    def smooth_setup(row, chunk):
        for k, count in enumerate(near_rows(wet, row, chunk, 1)):
            for tile in tiles:
                water = get(wet, tile, row + k)
                scale = water * (helm[tile, row + k] + count[tile]) + (1.0 - water)
                inverse = 0.8 / scale
                start = inverse * rhs[tile, row + k]
                diag[tile, row + k] = scale
                base[tile, row + k] = start
                gain[tile, row + k] = inverse * water
                put(flow, tile, row + k, water * start)

    rows_loop(2, 58, 14, smooth_setup)

    def smooth_second(row, chunk):
        for k, near in enumerate(near_rows(flow, row, chunk, 1)):
            for tile in tiles:
                value = 1.2 * base[tile, row + k] + gain[tile, row + k] * near[tile]
                state[tile, row + k] = value
                put(flow_next, tile, row + k, get(wet, tile, row + k) * value)

    rows_loop(3, 57, 18, smooth_second)

    def pair_sum(value):
        value = value + jnp.where(
            level % 2 == 0, pltpu.roll(value, CZ - 1, 0), pltpu.roll(value, 1, 0)
        )
        return value + jnp.where(
            lane % 2 == 0, pltpu.roll(value, LANES - 1, 1), pltpu.roll(value, 1, 1)
        )

    def coarse_mask(row, chunk):
        for k in range(chunk):
            for tile in tiles:
                fine = 2 * (row + k)
                total = pair_sum(get(wet, tile, fine) + get(wet, tile, fine + 1))
                put(wet_c, tile, row + k, jnp.where(total >= 3.5, 1.0, 0.0))

    rows_loop(1, 29, 14, coarse_mask)

    low, high = eig_ref[0], eig_ref[1]
    centre = 0.5 * (high + low)
    half = 0.5 * (high - low)
    sigma = centre / half
    rho = 1.0 / sigma
    start_scale = 1.0 / centre

    def coarse_setup(row, chunk):
        fine_near = near_rows(flow_next, 2 * row, 2 * chunk, 1)
        for k, count_c in enumerate(near_rows(wet_c, row, chunk, 2)):
            source, shift = [zero, zero], [zero, zero]
            for fine in (2 * (row + k), 2 * (row + k) + 1):
                near = next(fine_near)
                for tile in tiles:
                    left_over = rhs[tile, fine] - diag[tile, fine] * state[tile, fine]
                    source[tile] += get(wet, tile, fine) * (left_over + near[tile])
                    shift[tile] += helm[tile, fine]
            for tile in tiles:
                first_sum = 0.125 * pair_sum(source[tile])
                water_c = get(wet_c, tile, row + k)
                scale = water_c * (0.125 * pair_sum(shift[tile]) + 0.25 * count_c[tile])
                scale = scale + (1.0 - water_c)
                inverse = 1.0 / scale
                first = first_sum * inverse * start_scale
                diag_c[tile, row + k] = scale
                inverse_c[tile, row + k] = inverse
                remain[tile, row + k] = first_sum
                error[tile, row + k] = first
                direction[tile, row + k] = first
                put(masked, tile, row + k, water_c * first)

    rows_loop(2, 28, 13, coarse_setup)

    now, later = masked, masked_next
    for sweep in range(1, CHEB):
        rho_next = 1.0 / (2.0 * sigma - rho)
        keep = rho_next * rho
        add = 2.0 * rho_next / half

        def chebyshev(row, chunk, keep=keep, add=add, now=now, later=later):
            for k, near in enumerate(near_rows(now, row, chunk, 2)):
                for tile in tiles:
                    old = direction[tile, row + k]
                    water_c = get(wet_c, tile, row + k)
                    image = diag_c[tile, row + k] * old - 0.25 * water_c * near[tile]
                    left_over = remain[tile, row + k] - image
                    fresh = keep * old + add * (left_over * inverse_c[tile, row + k])
                    remain[tile, row + k] = left_over
                    direction[tile, row + k] = fresh
                    error[tile, row + k] = error[tile, row + k] + fresh
                    put(later, tile, row + k, water_c * fresh)

        rows_loop(2 + sweep, 28 - sweep, 13 - sweep, chebyshev)
        rho = rho_next
        now, later = later, now

    def spread(row, chunk):
        for k in range(chunk):
            value = [error[tile, row + k] for tile in tiles]
            sides = beside(value[0], value[1], 1)
            for tile in tiles:
                line = 0.75 * value[tile] + 0.25 * jnp.where(
                    lane % 2 == 0, sides[tile][0], sides[tile][1]
                )
                other = jnp.where(level % 2 == 0, pltpu.roll(line, 1, 0), pltpu.roll(line, CZ - 1, 0))
                other = jnp.where((level == 0) | (level == CZ - 1), 0.0, other)
                direction[tile, row + k] = 0.75 * line + 0.25 * other

    rows_loop(5, 25, 10, spread)

    def correct(row, chunk):
        for k in range(chunk):
            for tile in tiles:
                here = 0.75 * direction[tile, row + k]
                for fine, side in ((2 * (row + k), row + k - 1), (2 * (row + k) + 1, row + k + 1)):
                    water = get(wet, tile, fine)
                    value = state[tile, fine] + water * (here + 0.25 * direction[tile, side])
                    state[tile, fine] = value
                    put(flow, tile, fine, water * value)

    rows_loop(5, 25, 10, correct)

    def smooth(now, later):
        def step(row, chunk):
            for k, near in enumerate(near_rows(now, row, chunk, 1)):
                for tile in tiles:
                    value = 0.2 * state[tile, row + k] + base[tile, row + k]
                    value = value + gain[tile, row + k] * near[tile]
                    state[tile, row + k] = value
                    put(later, tile, row + k, get(wet, tile, row + k) * value)

        return step

    rows_loop(12, 48, 12, smooth(flow, flow_next))
    rows_loop(13, 47, 17, smooth(flow_next, flow))

    def finish_pressure(row, chunk):
        for k in range(chunk):
            pressure_ref[pl.ds(row + k - RIM, CZ, stride=ROWS), :] = state[0, row + k]

    rows_loop(RIM, RIM + ROWS, 16, finish_pressure)
    pressure_copy = pltpu.make_async_copy(pressure_ref, pressure_out, out_sem.at[0])
    pressure_copy.start()

    def finish(row, chunk):
        for k, near in enumerate(near_rows(flow, row, chunk, 1)):
            left_over = rhs[0, row + k] - diag[0, row + k] * state[0, row + k]
            left_over = left_over + get(wet, 0, row + k) * near[0]
            residual_ref[pl.ds(row + k - RIM, CZ, stride=ROWS), :] = left_over

    rows_loop(RIM, RIM + ROWS, 16, finish)
    residual_copy = pltpu.make_async_copy(residual_ref, residual_out, out_sem.at[1])
    residual_copy.start()
    pressure_copy.wait()
    residual_copy.wait()


def swapped(array, axis, first):
    pairs = [(i, i + 1) for i in range(first, lax.axis_size(axis) - 1, 2)]
    return lax.ppermute(array, axis, pairs + [(j, i) for i, j in pairs])


def in_hbm(array):
    return pltpu.with_memory_space_constraint(array, pltpu.HBM)


def f32(*shape):
    return jax.ShapeDtypeStruct(shape, jnp.float32)


def body(right_side, wet_mask, helmholtz, eig_low, eig_high):
    flat = (CZ * ROWS, LANES)
    right_flat = right_side.reshape(flat)
    mask_flat = wet_mask.reshape(flat)
    helm_flat = helmholtz.reshape(flat)
    limits = pltpu.CompilerParams(vmem_limit_bytes=24 * 1024 * 1024)

    far, near, own = pl.pallas_call(
        strips_kernel,
        out_shape=(f32(STRIP, CZ, LANES), f32(STRIP, CZ, LANES), f32(3, ROWS, CZ, LANES)),
        in_specs=[HBM] * 3,
        out_specs=(VMEM,) * 3,
        scratch_shapes=[
            pltpu.VMEM(flat, jnp.int32),
            pltpu.VMEM(flat, jnp.float32),
            pltpu.VMEM(flat, jnp.float32),
            pltpu.SemaphoreType.DMA((3,)),
        ],
        compiler_params=limits,
        name="strips",
    )(in_hbm(right_flat), in_hbm(mask_flat), in_hbm(helm_flat))
    far = swapped(far, "wide", 1)
    near = swapped(near, "wide", 0)

    tall, far, near, eigs = pl.pallas_call(
        sides_kernel,
        out_shape=(
            f32(3, TALL, CZ, LANES),
            f32(3 * PACKED, CZ, LANES),
            f32(3 * PACKED, CZ, LANES),
            f32(2, CZ, LANES),
        ),
        in_specs=[SMEM] * 2 + [VMEM] * 3,
        out_specs=(VMEM,) * 4,
        compiler_params=limits,
        name="sides",
    )(eig_low, eig_high, own, far, near)
    far = swapped(far, "narrow", 1)
    near = swapped(near, "narrow", 0)

    pressure, residual = pl.pallas_call(
        cycle_kernel,
        out_shape=(f32(*flat),) * 2,
        in_specs=[VMEM] * 4,
        out_specs=(HBM,) * 2,
        scratch_shapes=[pltpu.VMEM((2, TALL * PITCH + CZ, LANES), jnp.float32)] * 3
        + [pltpu.VMEM((2, TALL, CZ, LANES), jnp.float32)] * 6
        + [pltpu.VMEM((2, TALL // 2 * PITCH + CZ, LANES), jnp.float32)] * 3
        + [pltpu.VMEM((2, TALL // 2, CZ, LANES), jnp.float32)] * 5
        + [pltpu.VMEM(flat, jnp.float32)] * 2
        + [pltpu.SemaphoreType.DMA((2,))],
        compiler_params=limits,
        name="cycle",
    )(eigs, tall, far, near)
    shape = (CZ, ROWS, LANES)
    return pressure.reshape(shape), residual.reshape(shape)


def solution(mesh):
    field = P(None, "wide", "narrow")
    return jax.shard_map(
        body,
        mesh=mesh,
        in_specs=(field, field, field, P(), P()),
        out_specs=(field, field),
        check_vma=False,
    )
```

```python
import functools

import jax
import jax.numpy as jnp
from jax import lax
from jax.experimental import pallas as pl
from jax.experimental.pallas import tpu as pltpu
from jax.sharding import PartitionSpec as P

CHEB = 4

CZ = 8
ROWS = 32
LANES = 128
RIM = 14
TALL = ROWS + 2 * RIM
MASK_RIM = 13
RIGHT_RIM = 12
STRIP = MASK_RIM + 2 * RIGHT_RIM
SIDE = 16
GROUP = LANES // SIDE
PACKED = 8
PITCH = 2 * CZ

VMEM = pl.BlockSpec(memory_space=pltpu.VMEM)
SMEM = pl.BlockSpec(memory_space=pltpu.SMEM)
HBM = pl.BlockSpec(memory_space=pltpu.HBM)


def brick_row(ref, row):
    return ref[pl.ds(row, CZ, stride=ROWS), :]


def strips_kernel(
    right_hbm, mask_hbm, helm_hbm, far_ref, near_ref, own_ref, mask_ref, helm_ref, right_ref, sem
):
    odd = lax.rem(lax.axis_index("wide"), 2)
    copies = [
        pltpu.make_async_copy(source, dest, sem.at[k])
        for k, (source, dest) in enumerate(
            ((mask_hbm, mask_ref), (helm_hbm, helm_ref), (right_hbm, right_ref))
        )
    ]
    for copy in copies:
        copy.start()
    for field, (ref, rim, offset) in enumerate(
        (
            (mask_ref, MASK_RIM, 0),
            (helm_ref, RIGHT_RIM, MASK_RIM),
            (right_ref, RIGHT_RIM, MASK_RIM + RIGHT_RIM),
        )
    ):
        copies[field].wait()
        for row in range(ROWS):
            line = brick_row(ref, row).astype(jnp.float32)
            own_ref[field, row] = line
        to_far, to_near = (ROWS - rim) * odd, (ROWS - rim) * (1 - odd)
        for row in range(rim):
            far_ref[offset + row] = own_ref[field, to_far + row]
            near_ref[offset + row] = own_ref[field, to_near + row]


def sides_kernel(
    low_ref, high_ref, own_ref, far_ref, near_ref, tall_ref, far_out, near_out, eig_ref
):
    odd = lax.rem(lax.axis_index("wide"), 2)
    odd_column = lax.rem(lax.axis_index("narrow"), 2) == 1
    eig_ref[0] = jnp.full((CZ, LANES), low_ref[0], jnp.float32)
    eig_ref[1] = jnp.full((CZ, LANES), high_ref[0], jnp.float32)
    zero = jnp.zeros((CZ, LANES), jnp.float32)
    lane = lax.broadcasted_iota(jnp.int32, (CZ, LANES), 1)
    for field, offset, rim in (
        (0, 0, MASK_RIM),
        (1, MASK_RIM, RIGHT_RIM),
        (2, MASK_RIM + RIGHT_RIM, RIGHT_RIM),
    ):
        for row in (0, 1, TALL - 2, TALL - 1):
            tall_ref[field, row] = zero
        from_far = RIM - rim + (ROWS + rim) * odd
        from_near = RIM - rim + (ROWS + rim) * (1 - odd)
        for row in range(rim):
            tall_ref[field, from_far + row] = far_ref[offset + row]
            tall_ref[field, from_near + row] = near_ref[offset + row]
        for row in range(ROWS):
            tall_ref[field, RIM + row] = own_ref[field, row]

    def pack(first_group, groups):
        for i in range(groups):
            group = first_group + i
            for field in range(3):
                first, last = [], []
                for k in range(GROUP):
                    line = tall_ref[field, jnp.minimum(group * GROUP + k, TALL - 1)]
                    here = (lane >= SIDE * k) & (lane < SIDE * (k + 1))
                    one = pltpu.roll(line, SIDE * k, 1) if k else line
                    two = pltpu.roll(line, SIDE * (k + 1), 1) if k + 1 < GROUP else line
                    first.append(jnp.where(here, one, 0.0))
                    last.append(jnp.where(here, two, 0.0))
                while len(first) > 1:
                    first = [x + y for x, y in zip(first[::2], first[1::2])]
                    last = [x + y for x, y in zip(last[::2], last[1::2])]
                place = field * PACKED + group
                far_out[place] = jnp.where(odd_column, last[0], first[0])
                near_out[place] = jnp.where(odd_column, first[0], last[0])

    rows_loop(0, PACKED, 2, pack)


def rows_loop(start, stop, chunk, step):
    count = (stop - start) // chunk
    assert count * chunk == stop - start

    if count == 1:
        step(start, chunk)
        return

    def body(index, carry):
        step(start + index * chunk, chunk)
        return carry

    lax.fori_loop(0, count, body, 0)


def cycle_kernel(
    eig_ref,
    tall_ref,
    far_ref,
    near_ref,
    pressure_out,
    residual_out,
    wet,
    flow,
    flow_next,
    helm_side,
    rhs_side,
    diag,
    base,
    gain,
    state,
    wet_c,
    masked,
    masked_next,
    diag_c,
    inverse_c,
    remain,
    error,
    direction,
    pressure_ref,
    residual_ref,
    out_sem,
):
    lane = lax.broadcasted_iota(jnp.int32, (CZ, LANES), 1)
    level = lax.broadcasted_iota(jnp.int32, (CZ, LANES), 0)
    zero = jnp.zeros((CZ, LANES), jnp.float32)
    tiles = (0, 1)

    def put(ref, tile, row, value):
        ref[tile, pl.ds(row * PITCH + CZ, CZ), :] = value

    def get(ref, tile, row, shift=0):
        return ref[tile, pl.ds(row * PITCH + (CZ + shift), CZ), :]

    def clear(ref, count, reach):
        for place in [CZ - 1 - k for k in range(reach)] + [2 * CZ + k for k in range(reach)]:
            for first in range(0, count, CZ):
                first = min(first, count - CZ)
                for tile in tiles:
                    ref[tile, pl.ds(first * PITCH + place, CZ, stride=PITCH), :] = zero

    for ref in (wet, flow, flow_next):
        clear(ref, TALL, 1)
    for ref in (wet_c, masked, masked_next):
        clear(ref, TALL // 2, 2)

    def beside(main, side, reach):
        low, high = lane < reach, lane >= LANES - reach
        main_up, side_up = pltpu.roll(main, reach, 1), pltpu.roll(side, reach, 1)
        main_down = pltpu.roll(main, LANES - reach, 1)
        side_down = pltpu.roll(side, LANES - reach, 1)
        return (
            (jnp.where(low, side_up, main_up), jnp.where(high, side_down, main_down)),
            (jnp.where(low, main_up, side_up), jnp.where(high, main_down, side_down)),
        )

    def near_rows(ref, row, count, reach):
        lines = [[get(ref, tile, row + k - 1) for tile in tiles] for k in range(2)]
        for k in range(count):
            lines.append([get(ref, tile, row + k + 1) for tile in tiles])
            here = lines[k + 1]
            sides = beside(here[0], here[1], reach)
            yield [
                (lines[k][tile] + lines[k + 2][tile])
                + (get(ref, tile, row + k, -reach) + get(ref, tile, row + k, reach))
                + (sides[tile][0] + sides[tile][1])
                for tile in tiles
            ]

    odd_column = lax.rem(lax.axis_index("narrow"), 2) == 1

    def unpack(first_group, groups):
        for i in range(groups):
            group = first_group + i
            for field in range(3):
                far, near = far_ref[field * PACKED + group], near_ref[field * PACKED + group]
                after = jnp.where(odd_column, far, near)
                ahead = pltpu.roll(jnp.where(odd_column, near, far), LANES - SIDE, 1)
                for k in range(GROUP):
                    row = jnp.minimum(group * GROUP + k, TALL - 1)
                    low, high = SIDE * k, SIDE * (k + 1)
                    beyond = (low - SIDE) % LANES
                    both = jnp.where((lane >= beyond) & (lane < beyond + SIDE), ahead, 0.0)
                    both = jnp.where((lane >= low) & (lane < high), after, both)
                    if k:
                        both = pltpu.roll(both, LANES - low, 1)
                    if field == 0:
                        put(wet, 0, row, tall_ref[0, row])
                        put(wet, 1, row, both)
                    else:
                        (helm_side, rhs_side)[field - 1][row] = both

    rows_loop(0, PACKED, 4, unpack)

    def helm(tile, row):
        return helm_side[row] if tile else tall_ref[1, row]

    def rhs(tile, row):
        return rhs_side[row] if tile else tall_ref[2, row]

    def smooth_setup(row, chunk):
        for k, count in enumerate(near_rows(wet, row, chunk, 1)):
            for tile in tiles:
                water = get(wet, tile, row + k)
                scale = water * (helm(tile, row + k) + count[tile]) + (1.0 - water)
                inverse = 0.8 / scale
                start = inverse * rhs(tile, row + k)
                diag[tile, row + k] = scale
                base[tile, row + k] = start
                gain[tile, row + k] = inverse * water
                put(flow, tile, row + k, water * start)

    rows_loop(2, 58, 28, smooth_setup)

    def smooth_second(row, chunk):
        for k, near in enumerate(near_rows(flow, row, chunk, 1)):
            for tile in tiles:
                value = 1.2 * base[tile, row + k] + gain[tile, row + k] * near[tile]
                state[tile, row + k] = value
                put(flow_next, tile, row + k, get(wet, tile, row + k) * value)

    rows_loop(3, 57, 27, smooth_second)

    def pair_sum(value):
        value = value + jnp.where(
            level % 2 == 0, pltpu.roll(value, CZ - 1, 0), pltpu.roll(value, 1, 0)
        )
        return value + jnp.where(
            lane % 2 == 0, pltpu.roll(value, LANES - 1, 1), pltpu.roll(value, 1, 1)
        )

    def coarse_mask(row, chunk):
        for k in range(chunk):
            for tile in tiles:
                fine = 2 * (row + k)
                total = pair_sum(get(wet, tile, fine) + get(wet, tile, fine + 1))
                put(wet_c, tile, row + k, jnp.where(total >= 3.5, 1.0, 0.0))

    rows_loop(1, 29, 28, coarse_mask)

    low, high = eig_ref[0], eig_ref[1]
    centre = 0.5 * (high + low)
    half = 0.5 * (high - low)
    sigma = centre / half
    rho = 1.0 / sigma
    start_scale = 1.0 / centre

    def coarse_setup(row, chunk):
        fine_near = near_rows(flow_next, 2 * row, 2 * chunk, 1)
        for k, count_c in enumerate(near_rows(wet_c, row, chunk, 2)):
            source, shift = [zero, zero], [zero, zero]
            for fine in (2 * (row + k), 2 * (row + k) + 1):
                near = next(fine_near)
                for tile in tiles:
                    left_over = rhs(tile, fine) - diag[tile, fine] * state[tile, fine]
                    source[tile] += get(wet, tile, fine) * (left_over + near[tile])
                    shift[tile] += helm(tile, fine)
            for tile in tiles:
                first_sum = 0.125 * pair_sum(source[tile])
                water_c = get(wet_c, tile, row + k)
                scale = water_c * (0.125 * pair_sum(shift[tile]) + 0.25 * count_c[tile])
                scale = scale + (1.0 - water_c)
                inverse = 1.0 / scale
                first = first_sum * inverse * start_scale
                diag_c[tile, row + k] = scale
                inverse_c[tile, row + k] = inverse
                remain[tile, row + k] = first_sum
                error[tile, row + k] = first
                direction[tile, row + k] = first
                put(masked, tile, row + k, water_c * first)

    rows_loop(2, 28, 13, coarse_setup)

    now, later = masked, masked_next
    for sweep in range(1, CHEB):
        rho_next = 1.0 / (2.0 * sigma - rho)
        keep = rho_next * rho
        add = 2.0 * rho_next / half

        def chebyshev(row, chunk, keep=keep, add=add, now=now, later=later):
            for k, near in enumerate(near_rows(now, row, chunk, 2)):
                for tile in tiles:
                    old = direction[tile, row + k]
                    water_c = get(wet_c, tile, row + k)
                    image = diag_c[tile, row + k] * old - 0.25 * water_c * near[tile]
                    left_over = remain[tile, row + k] - image
                    fresh = keep * old + add * (left_over * inverse_c[tile, row + k])
                    remain[tile, row + k] = left_over
                    direction[tile, row + k] = fresh
                    error[tile, row + k] = error[tile, row + k] + fresh
                    put(later, tile, row + k, water_c * fresh)

        rows_loop(2 + sweep, 28 - sweep, 26 - 2 * sweep, chebyshev)
        rho = rho_next
        now, later = later, now

    def spread(row, chunk):
        for k in range(chunk):
            value = [error[tile, row + k] for tile in tiles]
            sides = beside(value[0], value[1], 1)
            for tile in tiles:
                line = 0.75 * value[tile] + 0.25 * jnp.where(
                    lane % 2 == 0, sides[tile][0], sides[tile][1]
                )
                other = jnp.where(level % 2 == 0, pltpu.roll(line, 1, 0), pltpu.roll(line, CZ - 1, 0))
                other = jnp.where((level == 0) | (level == CZ - 1), 0.0, other)
                direction[tile, row + k] = 0.75 * line + 0.25 * other

    rows_loop(5, 25, 20, spread)

    def correct(row, chunk):
        for k in range(chunk):
            for tile in tiles:
                here = 0.75 * direction[tile, row + k]
                for fine, side in ((2 * (row + k), row + k - 1), (2 * (row + k) + 1, row + k + 1)):
                    water = get(wet, tile, fine)
                    value = state[tile, fine] + water * (here + 0.25 * direction[tile, side])
                    state[tile, fine] = value
                    put(flow, tile, fine, water * value)

    rows_loop(5, 25, 20, correct)

    def smooth(now, later, last=False):
        def step(row, chunk):
            for k, near in enumerate(near_rows(now, row, chunk, 1)):
                for tile in tiles:
                    value = 0.2 * state[tile, row + k] + base[tile, row + k]
                    value = value + gain[tile, row + k] * near[tile]
                    state[tile, row + k] = value
                    put(later, tile, row + k, get(wet, tile, row + k) * value)
                    if last and tile == 0 and RIM <= row + k < RIM + ROWS:
                        pressure_ref[pl.ds(row + k - RIM, CZ, stride=ROWS), :] = value

        return step

    rows_loop(12, 48, 18, smooth(flow, flow_next))
    rows_loop(13, 47, 34, smooth(flow_next, flow, True))

    pressure_copy = pltpu.make_async_copy(pressure_ref, pressure_out, out_sem.at[0])
    pressure_copy.start()

    def finish(row, chunk):
        for k, near in enumerate(near_rows(flow, row, chunk, 1)):
            left_over = rhs(0, row + k) - diag[0, row + k] * state[0, row + k]
            left_over = left_over + get(wet, 0, row + k) * near[0]
            residual_ref[pl.ds(row + k - RIM, CZ, stride=ROWS), :] = left_over

    rows_loop(RIM, RIM + ROWS, 32, finish)
    residual_copy = pltpu.make_async_copy(residual_ref, residual_out, out_sem.at[1])
    residual_copy.start()
    pressure_copy.wait()
    residual_copy.wait()


def swapped(array, axis, first):
    pairs = [(i, i + 1) for i in range(first, lax.axis_size(axis) - 1, 2)]
    return lax.ppermute(array, axis, pairs + [(j, i) for i, j in pairs])


def in_hbm(array):
    return pltpu.with_memory_space_constraint(array, pltpu.HBM)


def f32(*shape):
    return jax.ShapeDtypeStruct(shape, jnp.float32)


def body(right_side, wet_mask, helmholtz, eig_low, eig_high):
    flat = (CZ * ROWS, LANES)
    right_flat = right_side.reshape(flat)
    mask_flat = wet_mask.reshape(flat)
    helm_flat = helmholtz.reshape(flat)
    limits = pltpu.CompilerParams(vmem_limit_bytes=24 * 1024 * 1024)

    far, near, own = pl.pallas_call(
        strips_kernel,
        out_shape=(f32(STRIP, CZ, LANES), f32(STRIP, CZ, LANES), f32(3, ROWS, CZ, LANES)),
        in_specs=[HBM] * 3,
        out_specs=(VMEM,) * 3,
        scratch_shapes=[
            pltpu.VMEM(flat, jnp.int32),
            pltpu.VMEM(flat, jnp.float32),
            pltpu.VMEM(flat, jnp.float32),
            pltpu.SemaphoreType.DMA((3,)),
        ],
        compiler_params=limits,
        name="strips",
    )(in_hbm(right_flat), in_hbm(mask_flat), in_hbm(helm_flat))
    far = swapped(far, "wide", 1)
    near = swapped(near, "wide", 0)

    tall, far, near, eigs = pl.pallas_call(
        sides_kernel,
        out_shape=(
            f32(3, TALL, CZ, LANES),
            f32(3 * PACKED, CZ, LANES),
            f32(3 * PACKED, CZ, LANES),
            f32(2, CZ, LANES),
        ),
        in_specs=[SMEM] * 2 + [VMEM] * 3,
        out_specs=(VMEM,) * 4,
        compiler_params=limits,
        name="sides",
    )(eig_low, eig_high, own, far, near)
    far = swapped(far, "narrow", 1)
    near = swapped(near, "narrow", 0)

    pressure, residual = pl.pallas_call(
        cycle_kernel,
        out_shape=(f32(*flat),) * 2,
        in_specs=[VMEM] * 4,
        out_specs=(HBM,) * 2,
        scratch_shapes=[pltpu.VMEM((2, TALL * PITCH + 2 * CZ, LANES), jnp.float32)] * 3
        + [pltpu.VMEM((TALL, CZ, LANES), jnp.float32)] * 2
        + [pltpu.VMEM((2, TALL, CZ, LANES), jnp.float32)] * 4
        + [pltpu.VMEM((2, TALL // 2 * PITCH + 2 * CZ, LANES), jnp.float32)] * 3
        + [pltpu.VMEM((2, TALL // 2, CZ, LANES), jnp.float32)] * 5
        + [pltpu.VMEM(flat, jnp.float32)] * 2
        + [pltpu.SemaphoreType.DMA((2,))],
        compiler_params=limits,
        name="cycle",
    )(eigs, tall, far, near)
    shape = (CZ, ROWS, LANES)
    return pressure.reshape(shape), residual.reshape(shape)


def solution(mesh):
    field = P(None, "wide", "narrow")
    return jax.shard_map(
        body,
        mesh=mesh,
        in_specs=(field, field, field, P(), P()),
        out_specs=(field, field),
        check_vma=False,
    )
```

```python
import functools

import jax
import jax.numpy as jnp
from jax import lax
from jax.experimental import pallas as pl
from jax.experimental.pallas import tpu as pltpu
from jax.sharding import PartitionSpec as P

CHEB = 4

CZ = 8
ROWS = 32
LANES = 128
RIM = 14
TALL = ROWS + 2 * RIM + 4
MASK_RIM = 13
RIGHT_RIM = 12
STRIP = MASK_RIM + 2 * RIGHT_RIM
SIDE = 16
SPAN = 2 * SIDE
BLOCK = TALL * SPAN // LANES
PACKED = BLOCK // 2
PITCH = 2 * CZ

VMEM = pl.BlockSpec(memory_space=pltpu.VMEM)
SMEM = pl.BlockSpec(memory_space=pltpu.SMEM)
HBM = pl.BlockSpec(memory_space=pltpu.HBM)


def brick_row(ref, row):
    return ref[pl.ds(row, CZ, stride=ROWS), :]


def strips_kernel(
    right_hbm, mask_hbm, helm_hbm, far_ref, near_ref, own_ref, mask_ref, helm_ref, right_ref, sem
):
    odd = lax.rem(lax.axis_index("wide"), 2)
    copies = [
        pltpu.make_async_copy(source, dest, sem.at[k])
        for k, (source, dest) in enumerate(
            ((mask_hbm, mask_ref), (helm_hbm, helm_ref), (right_hbm, right_ref))
        )
    ]
    for copy in copies:
        copy.start()
    for field, (ref, rim, offset) in enumerate(
        (
            (mask_ref, MASK_RIM, 0),
            (helm_ref, RIGHT_RIM, MASK_RIM),
            (right_ref, RIGHT_RIM, MASK_RIM + RIGHT_RIM),
        )
    ):
        copies[field].wait()
        for row in range(ROWS):
            line = brick_row(ref, row).astype(jnp.float32)
            own_ref[field, row] = line
        to_far, to_near = (ROWS - rim) * odd, (ROWS - rim) * (1 - odd)
        for row in range(rim):
            far_ref[offset + row] = own_ref[field, to_far + row]
            near_ref[offset + row] = own_ref[field, to_near + row]


def sides_kernel(
    low_ref, high_ref, own_ref, far_ref, near_ref, tall_ref, far_out, near_out, eig_ref
):
    odd = lax.rem(lax.axis_index("wide"), 2)
    odd_column = lax.rem(lax.axis_index("narrow"), 2) == 1
    eig_ref[0] = jnp.full((CZ, LANES), low_ref[0], jnp.float32)
    eig_ref[1] = jnp.full((CZ, LANES), high_ref[0], jnp.float32)
    zero = jnp.zeros((CZ, LANES), jnp.float32)
    lane = lax.broadcasted_iota(jnp.int32, (CZ, LANES), 1)
    for field, offset, rim in (
        (0, 0, MASK_RIM),
        (1, MASK_RIM, RIGHT_RIM),
        (2, MASK_RIM + RIGHT_RIM, RIGHT_RIM),
    ):
        for row in (0, 1) + tuple(range(TALL - 6, TALL)):
            tall_ref[field, row] = zero
        from_far = RIM - rim + (ROWS + rim) * odd
        from_near = RIM - rim + (ROWS + rim) * (1 - odd)
        for row in range(rim):
            tall_ref[field, from_far + row] = far_ref[offset + row]
            tall_ref[field, from_near + row] = near_ref[offset + row]
        for row in range(ROWS):
            tall_ref[field, RIM + row] = own_ref[field, row]

    block, half = lane // SPAN, lane % SPAN < SIDE
    for field in range(3):
        for i in range(BLOCK // 2):
            first, last = zero, zero
            for b in range(LANES // SPAN):
                low = tall_ref[field, BLOCK * b + i]
                low = pltpu.roll(low, SPAN * b + SIDE, 1)
                high = tall_ref[field, BLOCK * b + i + BLOCK // 2]
                high = pltpu.roll(high, SPAN * (b + 1), 1) if SPAN * (b + 1) < LANES else high
                here, after = block == b, block == (b + 1) % (LANES // SPAN)
                last = jnp.where(here, jnp.where(half, low, high), last)
                first = jnp.where(here & ~half, low, jnp.where(after & half, high, first))
            place = field * PACKED + i
            far_out[place] = jnp.where(odd_column, last, first)
            near_out[place] = jnp.where(odd_column, first, last)


class Field:
    def __init__(self, main, side, height):
        self.refs, self.height = (main, side), height

    def get(self, kind, row, shift=0):
        return self.refs[kind][row]

    def put(self, kind, row, value):
        self.refs[kind][row] = value

    def line(self, kind, row):
        if kind and row < 0:
            return pltpu.roll(self.get(1, self.height - 1), SPAN, 1)
        if kind and row == self.height:
            return pltpu.roll(self.get(1, 0), LANES - SPAN, 1)
        return self.get(kind, row)


class Padded(Field):
    def get(self, kind, row, shift=0):
        return self.refs[kind][pl.ds(row * PITCH + CZ + shift, CZ), :]

    def put(self, kind, row, value):
        self.refs[kind][pl.ds(row * PITCH + CZ, CZ), :] = value

    def clear(self, reach):
        zero = jnp.zeros((CZ, LANES), jnp.float32)
        for ref, count in zip(self.refs, (self.height * (LANES // SPAN), self.height)):
            for place in [CZ - 1 - k for k in range(reach)] + [2 * CZ + k for k in range(reach)]:
                for first in range(0, count, CZ):
                    ref[pl.ds(first * PITCH + place, CZ, stride=PITCH), :] = zero


def cycle_kernel(eig_ref, tall_ref, far_ref, near_ref, pressure_out, residual_out, *scratch):
    scratch = list(scratch)
    out_sem = scratch.pop()
    residual_ref, pressure_ref = scratch.pop(), scratch.pop()

    def fields(kind, height, count):
        return [kind(scratch.pop(0), scratch.pop(0), height) for _ in range(count)]

    wet, flow, flow_next = fields(Padded, BLOCK, 3)
    diag, base, gain, state = fields(Field, BLOCK, 4)
    wet_c, masked, masked_next = fields(Padded, BLOCK // 2, 3)
    diag_c, inverse_c, remain, error, spread = fields(Field, BLOCK // 2, 5)
    helm = Field(tall_ref.at[1], scratch.pop(0), BLOCK)
    rhs = Field(tall_ref.at[2], scratch.pop(0), BLOCK)

    lane = lax.broadcasted_iota(jnp.int32, (CZ, LANES), 1)
    level = lax.broadcasted_iota(jnp.int32, (CZ, LANES), 0)
    place = lane % SPAN
    blocks = [lane // SPAN == b for b in range(LANES // SPAN)]

    wet.clear(1)
    flow.clear(1)
    flow_next.clear(1)
    wet_c.clear(2)
    masked.clear(2)
    masked_next.clear(2)

    odd_column = lax.rem(lax.axis_index("narrow"), 2) == 1
    for row in range(1, TALL - 5):
        wet.put(0, row, tall_ref[0, row])
    for index, field in enumerate((wet, helm, rhs)):
        for i in range(BLOCK // 2):
            far, near = far_ref[index * PACKED + i], near_ref[index * PACKED + i]
            right = jnp.where(odd_column, far, near)
            left = jnp.where(odd_column, near, far)
            field.put(1, i, jnp.where(place < SIDE, left, right))
            late = jnp.where(place < SIDE, right, left)
            field.put(1, i + BLOCK // 2, pltpu.roll(late, LANES - SIDE, 1))

    def cells(start, stop, height):
        for i in range(height):
            rows = [(b, height * b + i) for b in range(LANES // SPAN)]
            yield i, [(b, row) for b, row in rows if start <= row < stop]

    def beside(mains, side, reach):
        edge = side
        found = []
        for b, main in mains:
            inner = pltpu.roll(side, (LANES - SIDE - SPAN * b) % LANES, 1)
            before = jnp.where(lane >= LANES - reach, inner, main)
            after = jnp.where(lane < reach, inner, main)
            found.append((pltpu.roll(before, reach, 1), pltpu.roll(after, LANES - reach, 1)))
            edge = jnp.where(blocks[b], pltpu.roll(main, SIDE + SPAN * b, 1), edge)
        before = jnp.where((place < SIDE) & (place >= SIDE - reach), edge, side)
        after = jnp.where((place >= SIDE) & (place < SIDE + reach), edge, side)
        found.append((pltpu.roll(before, reach, 1), pltpu.roll(after, LANES - reach, 1)))
        return found

    def near_rows(field, start, stop, reach):
        for i, rows in cells(start, stop, field.height):
            side = field.get(1, i)
            sides = beside([(b, field.get(0, row)) for b, row in rows], side, reach)
            out = []
            for (kind, row), (before, after) in zip([(0, r) for _, r in rows] + [(1, i)], sides):
                total = field.line(kind, row - 1) + field.line(kind, row + 1)
                total = total + (field.get(kind, row, -reach) + field.get(kind, row, reach))
                out.append((kind, row, total + (before + after)))
            yield out

    def flat_rows(start, stop, height):
        for i, rows in cells(start, stop, height):
            yield from [(0, row) for _, row in rows] + [(1, i)]

    for group in near_rows(wet, 2, 58, 1):
        for kind, row, count in group:
            water = wet.get(kind, row)
            scale = water * (helm.get(kind, row) + count) + (1.0 - water)
            inverse = 0.8 / scale
            start = inverse * rhs.get(kind, row)
            diag.put(kind, row, scale)
            base.put(kind, row, start)
            gain.put(kind, row, inverse * water)
            flow.put(kind, row, water * start)

    for group in near_rows(flow, 3, 57, 1):
        for kind, row, near in group:
            value = 1.2 * base.get(kind, row) + gain.get(kind, row) * near
            state.put(kind, row, value)
            flow_next.put(kind, row, wet.get(kind, row) * value)

    def pair_sum(value):
        value = value + jnp.where(
            level % 2 == 0, pltpu.roll(value, CZ - 1, 0), pltpu.roll(value, 1, 0)
        )
        return value + jnp.where(
            lane % 2 == 0, pltpu.roll(value, LANES - 1, 1), pltpu.roll(value, 1, 1)
        )

    for kind, row in flat_rows(1, 29, BLOCK // 2):
        total = pair_sum(wet.get(kind, 2 * row) + wet.get(kind, 2 * row + 1))
        wet_c.put(kind, row, jnp.where(total >= 3.5, 1.0, 0.0))

    low, high = eig_ref[0], eig_ref[1]
    centre = 0.5 * (high + low)
    half = 0.5 * (high - low)
    sigma = centre / half
    rho = 1.0 / sigma
    start_scale = 1.0 / centre

    fine_near = near_rows(flow_next, 4, 56, 1)
    for group in near_rows(wet_c, 2, 28, 2):
        parts = {}
        for _ in range(2):
            for kind, row, near in next(fine_near):
                left_over = rhs.get(kind, row) - diag.get(kind, row) * state.get(kind, row)
                left_over = wet.get(kind, row) * (left_over + near)
                lump = helm.get(kind, row)
                if (kind, row // 2) in parts:
                    left_over = left_over + parts[kind, row // 2][0]
                    lump = lump + parts[kind, row // 2][1]
                parts[kind, row // 2] = (left_over, lump)
        for kind, row, count_c in group:
            source, shift = (0.125 * pair_sum(part) for part in parts[kind, row])
            water_c = wet_c.get(kind, row)
            scale = water_c * (shift + 0.25 * count_c) + (1.0 - water_c)
            inverse = 1.0 / scale
            first = source * inverse * start_scale
            diag_c.put(kind, row, scale)
            inverse_c.put(kind, row, inverse)
            remain.put(kind, row, source)
            error.put(kind, row, first)
            spread.put(kind, row, first)
            masked.put(kind, row, water_c * first)

    direction, now, later = spread, masked, masked_next
    for sweep in range(1, CHEB):
        rho_next = 1.0 / (2.0 * sigma - rho)
        keep = rho_next * rho
        add = 2.0 * rho_next / half
        for group in near_rows(now, 2 + sweep, 28 - sweep, 2):
            for kind, row, near in group:
                old = direction.get(kind, row)
                water_c = wet_c.get(kind, row)
                image = diag_c.get(kind, row) * old - 0.25 * water_c * near
                left_over = remain.get(kind, row) - image
                fresh = keep * old + add * (left_over * inverse_c.get(kind, row))
                error.put(kind, row, error.get(kind, row) + fresh)
                if sweep + 1 < CHEB:
                    remain.put(kind, row, left_over)
                    direction.put(kind, row, fresh)
                    later.put(kind, row, water_c * fresh)
        rho = rho_next
        now, later = later, now

    for i, rows in cells(5, 25, BLOCK // 2):
        values = [error.get(0, row) for _, row in rows] + [error.get(1, i)]
        sides = beside([(b, error.get(0, row)) for b, row in rows], values[-1], 1)
        for k, (kind, row) in enumerate([(0, row) for _, row in rows] + [(1, i)]):
            line = 0.75 * values[k] + 0.25 * jnp.where(lane % 2 == 0, *sides[k])
            other = jnp.where(level % 2 == 0, pltpu.roll(line, 1, 0), pltpu.roll(line, CZ - 1, 0))
            other = jnp.where((level == 0) | (level == CZ - 1), 0.0, other)
            spread.put(kind, row, 0.75 * line + 0.25 * other)

    for kind, row in flat_rows(5, 25, BLOCK // 2):
        here = 0.75 * spread.get(kind, row)
        for fine, beyond in ((2 * row, row - 1), (2 * row + 1, row + 1)):
            if kind == 0 and not 11 <= fine < 49:
                continue
            water = wet.get(kind, fine)
            value = state.get(kind, fine) + water * (here + 0.25 * spread.line(kind, beyond))
            state.put(kind, fine, value)
            flow.put(kind, fine, water * value)

    for start, stop, now, later in ((12, 48, flow, flow_next), (13, 47, flow_next, flow)):
        for group in near_rows(now, start, stop, 1):
            for kind, row, near in group:
                value = 0.2 * state.get(kind, row) + base.get(kind, row)
                value = value + gain.get(kind, row) * near
                state.put(kind, row, value)
                later.put(kind, row, wet.get(kind, row) * value)
                if later is flow and kind == 0 and RIM <= row < RIM + ROWS:
                    pressure_ref[pl.ds(row - RIM, CZ, stride=ROWS), :] = value

    pressure_copy = pltpu.make_async_copy(pressure_ref, pressure_out, out_sem.at[0])
    pressure_copy.start()
    for group in near_rows(flow, RIM, RIM + ROWS, 1):
        for kind, row, near in group[:-1]:
            left_over = rhs.get(0, row) - diag.get(0, row) * state.get(0, row)
            left_over = left_over + wet.get(0, row) * near
            residual_ref[pl.ds(row - RIM, CZ, stride=ROWS), :] = left_over
    residual_copy = pltpu.make_async_copy(residual_ref, residual_out, out_sem.at[1])
    residual_copy.start()
    pressure_copy.wait()
    residual_copy.wait()


def swapped(array, axis, first):
    pairs = [(i, i + 1) for i in range(first, lax.axis_size(axis) - 1, 2)]
    return lax.ppermute(array, axis, pairs + [(j, i) for i, j in pairs])


def in_hbm(array):
    return pltpu.with_memory_space_constraint(array, pltpu.HBM)


def f32(*shape):
    return jax.ShapeDtypeStruct(shape, jnp.float32)


def body(right_side, wet_mask, helmholtz, eig_low, eig_high):
    flat = (CZ * ROWS, LANES)
    right_flat = right_side.reshape(flat)
    mask_flat = wet_mask.reshape(flat)
    helm_flat = helmholtz.reshape(flat)
    limits = pltpu.CompilerParams(vmem_limit_bytes=24 * 1024 * 1024)

    far, near, own = pl.pallas_call(
        strips_kernel,
        out_shape=(f32(STRIP, CZ, LANES), f32(STRIP, CZ, LANES), f32(3, ROWS, CZ, LANES)),
        in_specs=[HBM] * 3,
        out_specs=(VMEM,) * 3,
        scratch_shapes=[
            pltpu.VMEM(flat, jnp.int32),
            pltpu.VMEM(flat, jnp.float32),
            pltpu.VMEM(flat, jnp.float32),
            pltpu.SemaphoreType.DMA((3,)),
        ],
        compiler_params=limits,
        name="strips",
    )(in_hbm(right_flat), in_hbm(mask_flat), in_hbm(helm_flat))
    far = swapped(far, "wide", 1)
    near = swapped(near, "wide", 0)

    tall, far, near, eigs = pl.pallas_call(
        sides_kernel,
        out_shape=(
            f32(3, TALL, CZ, LANES),
            f32(3 * PACKED, CZ, LANES),
            f32(3 * PACKED, CZ, LANES),
            f32(2, CZ, LANES),
        ),
        in_specs=[SMEM] * 2 + [VMEM] * 3,
        out_specs=(VMEM,) * 4,
        compiler_params=limits,
        name="sides",
    )(eig_low, eig_high, own, far, near)
    far = swapped(far, "narrow", 1)
    near = swapped(near, "narrow", 0)

    padded = [((rows + 1) * PITCH, LANES) for rows in (TALL, BLOCK)]
    plain = [(rows, CZ, LANES) for rows in (TALL, BLOCK)]
    padded_c = [((rows // 2 + 1) * PITCH, LANES) for rows in (TALL, BLOCK)]
    plain_c = [(rows // 2, CZ, LANES) for rows in (TALL, BLOCK)]
    shapes = padded * 3 + plain * 4 + padded_c * 3 + plain_c * 5 + [plain[1]] * 2 + [flat] * 2
    pressure, residual = pl.pallas_call(
        cycle_kernel,
        out_shape=(f32(*flat),) * 2,
        in_specs=[VMEM] * 4,
        out_specs=(HBM,) * 2,
        scratch_shapes=[pltpu.VMEM(shape, jnp.float32) for shape in shapes]
        + [pltpu.SemaphoreType.DMA((2,))],
        compiler_params=limits,
        name="cycle",
    )(eigs, tall, far, near)
    shape = (CZ, ROWS, LANES)
    return pressure.reshape(shape), residual.reshape(shape)


def solution(mesh):
    field = P(None, "wide", "narrow")
    return jax.shard_map(
        body,
        mesh=mesh,
        in_specs=(field, field, field, P(), P()),
        out_specs=(field, field),
        check_vma=False,
    )
```

```python
import functools

import jax
import jax.numpy as jnp
from jax import lax
from jax.experimental import pallas as pl
from jax.experimental.pallas import tpu as pltpu
from jax.sharding import PartitionSpec as P

CHEB = 4

CZ = 8
ROWS = 32
LANES = 128
RIM = 14
TALL = ROWS + 2 * RIM + 4
MASK_RIM = 13
RIGHT_RIM = 12
STRIP = MASK_RIM + 2 * RIGHT_RIM
SIDE = 16
SPAN = 2 * SIDE
BLOCK = TALL * SPAN // LANES
BLOCKS = LANES // SPAN
ALL = tuple(range(BLOCKS))
PACKED = BLOCK // 2
PITCH = 2 * CZ

VMEM = pl.BlockSpec(memory_space=pltpu.VMEM)
SMEM = pl.BlockSpec(memory_space=pltpu.SMEM)
HBM = pl.BlockSpec(memory_space=pltpu.HBM)


def brick_row(ref, row):
    return ref[pl.ds(row, CZ, stride=ROWS), :]


def strips_kernel(
    right_hbm, mask_hbm, helm_hbm, far_ref, near_ref, own_ref, mask_ref, helm_ref, right_ref, sem
):
    odd = lax.rem(lax.axis_index("wide"), 2)
    copies = [
        pltpu.make_async_copy(source, dest, sem.at[k])
        for k, (source, dest) in enumerate(
            ((mask_hbm, mask_ref), (helm_hbm, helm_ref), (right_hbm, right_ref))
        )
    ]
    for copy in copies:
        copy.start()
    for field, (ref, rim, offset) in enumerate(
        (
            (mask_ref, MASK_RIM, 0),
            (helm_ref, RIGHT_RIM, MASK_RIM),
            (right_ref, RIGHT_RIM, MASK_RIM + RIGHT_RIM),
        )
    ):
        copies[field].wait()
        for row in range(ROWS):
            line = brick_row(ref, row).astype(jnp.float32)
            own_ref[field, row] = line
        to_far, to_near = (ROWS - rim) * odd, (ROWS - rim) * (1 - odd)
        for row in range(rim):
            far_ref[offset + row] = own_ref[field, to_far + row]
            near_ref[offset + row] = own_ref[field, to_near + row]


def sides_kernel(
    low_ref, high_ref, own_ref, far_ref, near_ref, tall_ref, far_out, near_out, eig_ref
):
    odd = lax.rem(lax.axis_index("wide"), 2)
    odd_column = lax.rem(lax.axis_index("narrow"), 2) == 1
    eig_ref[0] = jnp.full((CZ, LANES), low_ref[0], jnp.float32)
    eig_ref[1] = jnp.full((CZ, LANES), high_ref[0], jnp.float32)
    zero = jnp.zeros((CZ, LANES), jnp.float32)
    lane = lax.broadcasted_iota(jnp.int32, (CZ, LANES), 1)
    for field, offset, rim in (
        (0, 0, MASK_RIM),
        (1, MASK_RIM, RIGHT_RIM),
        (2, MASK_RIM + RIGHT_RIM, RIGHT_RIM),
    ):
        for row in (0, 1) + tuple(range(TALL - 6, TALL)):
            tall_ref[field, row] = zero
        from_far = RIM - rim + (ROWS + rim) * odd
        from_near = RIM - rim + (ROWS + rim) * (1 - odd)
        for row in range(rim):
            tall_ref[field, from_far + row] = far_ref[offset + row]
            tall_ref[field, from_near + row] = near_ref[offset + row]
        for row in range(ROWS):
            tall_ref[field, RIM + row] = own_ref[field, row]

    block, half = lane // SPAN, lane % SPAN < SIDE
    for field in range(3):
        for i in range(BLOCK // 2):
            first, last = zero, zero
            for b in range(LANES // SPAN):
                low = tall_ref[field, BLOCK * b + i]
                low = pltpu.roll(low, SPAN * b + SIDE, 1)
                high = tall_ref[field, BLOCK * b + i + BLOCK // 2]
                high = pltpu.roll(high, SPAN * (b + 1), 1) if SPAN * (b + 1) < LANES else high
                here, after = block == b, block == (b + 1) % (LANES // SPAN)
                last = jnp.where(here, jnp.where(half, low, high), last)
                first = jnp.where(here & ~half, low, jnp.where(after & half, high, first))
            place = field * PACKED + i
            far_out[place] = jnp.where(odd_column, last, first)
            near_out[place] = jnp.where(odd_column, first, last)


def rows_loop(start, stop, chunk, step):
    count = (stop - start) // chunk
    assert count * chunk == stop - start
    if count == 1:
        step(start, chunk)
        return

    def body(index, carry):
        step(start + index * chunk, chunk)
        return carry

    lax.fori_loop(0, count, body, 0)


class Field:
    def __init__(self, main, side, height, ahead=(1, 1)):
        self.refs, self.height, self.ahead = (main, side), height, ahead

    def get(self, kind, row, shift=0):
        return self.refs[kind][row + self.ahead[kind]]

    def put(self, kind, row, value):
        self.refs[kind][row + self.ahead[kind]] = value

    def wrap(self):
        self.put(1, -1, pltpu.roll(self.get(1, self.height - 1), SPAN, 1))
        self.put(1, self.height, pltpu.roll(self.get(1, 0), LANES - SPAN, 1))


class Padded(Field):
    def get(self, kind, row, shift=0):
        return self.refs[kind][pl.ds(row * PITCH + (PITCH + CZ + shift), CZ), :]

    def put(self, kind, row, value):
        self.refs[kind][pl.ds(row * PITCH + (PITCH + CZ), CZ), :] = value

    def clear(self, reach):
        zero = jnp.zeros((CZ, LANES), jnp.float32)
        for ref, count in zip(self.refs, (self.height * BLOCKS, self.height)):
            for place in [CZ - 1 - k for k in range(reach)] + [2 * CZ + k for k in range(reach)]:
                for first in range(0, count, CZ):
                    ref[pl.ds((first + 1) * PITCH + place, CZ, stride=PITCH), :] = zero


def cycle_kernel(eig_ref, tall_ref, far_ref, near_ref, pressure_out, residual_out, *scratch):
    scratch = list(scratch)
    out_sem = scratch.pop()
    residual_ref, pressure_ref = scratch.pop(), scratch.pop()

    def fields(kind, height, count):
        return [kind(scratch.pop(0), scratch.pop(0), height) for _ in range(count)]

    wet, flow, flow_next = fields(Padded, BLOCK, 3)
    diag, base, gain, state = fields(Field, BLOCK, 4)
    wet_c, masked, masked_next = fields(Padded, BLOCK // 2, 3)
    diag_c, inverse_c, remain, error, spread = fields(Field, BLOCK // 2, 5)
    helm = Field(tall_ref.at[1], scratch.pop(0), BLOCK, (0, 1))
    rhs = Field(tall_ref.at[2], scratch.pop(0), BLOCK, (0, 1))

    lane = lax.broadcasted_iota(jnp.int32, (CZ, LANES), 1)
    level = lax.broadcasted_iota(jnp.int32, (CZ, LANES), 0)
    place = lane % SPAN
    blocks = [lane // SPAN == b for b in range(BLOCKS)]

    wet.clear(1)
    flow.clear(1)
    flow_next.clear(1)
    wet_c.clear(2)
    masked.clear(2)
    masked_next.clear(2)

    odd_column = lax.rem(lax.axis_index("narrow"), 2) == 1

    def copy_wet(row, count):
        for k in range(count):
            wet.put(0, row + k, tall_ref[0, row + k])

    rows_loop(0, TALL, 16, copy_wet)

    def unpack(i, count):
        for k in range(count):
            for index, field in enumerate((wet, helm, rhs)):
                far, near = far_ref[index * PACKED + i + k], near_ref[index * PACKED + i + k]
                right = jnp.where(odd_column, far, near)
                left = jnp.where(odd_column, near, far)
                field.put(1, i + k, jnp.where(place < SIDE, left, right))
                late = jnp.where(place < SIDE, right, left)
                field.put(1, i + k + PACKED, pltpu.roll(late, LANES - SIDE, 1))

    rows_loop(0, PACKED, 4, unpack)
    wet.wrap()

    def cells(i, chosen, height):
        return [(0, height * b + i) for b in chosen] + [(1, i)]

    def beside(mains, side, reach):
        edge = side
        found = []
        for b, main in mains:
            inner = pltpu.roll(side, (LANES - SIDE - SPAN * b) % LANES, 1)
            before = jnp.where(lane >= LANES - reach, inner, main)
            after = jnp.where(lane < reach, inner, main)
            found.append((pltpu.roll(before, reach, 1), pltpu.roll(after, LANES - reach, 1)))
            edge = jnp.where(blocks[b], pltpu.roll(main, SIDE + SPAN * b, 1), edge)
        before = jnp.where((place < SIDE) & (place >= SIDE - reach), edge, side)
        after = jnp.where((place >= SIDE) & (place < SIDE + reach), edge, side)
        found.append((pltpu.roll(before, reach, 1), pltpu.roll(after, LANES - reach, 1)))
        return found

    def near_rows(field, i, count, reach, chosen=ALL):
        lines = [[field.get(*cell) for cell in cells(i + k, chosen, field.height)] for k in (-1, 0)]
        for k in range(count):
            lines.append([field.get(*cell) for cell in cells(i + k + 1, chosen, field.height)])
            here = lines[k + 1]
            sides = beside(list(zip(chosen, here)), here[-1], reach)
            out = []
            for n, (kind, row) in enumerate(cells(i + k, chosen, field.height)):
                total = lines[k][n] + lines[k + 2][n]
                total = total + (field.get(kind, row, -reach) + field.get(kind, row, reach))
                out.append((kind, row, total + (sides[n][0] + sides[n][1])))
            yield out

    def smooth_setup(i, count):
        for group in near_rows(wet, i, count, 1):
            for kind, row, around in group:
                water = wet.get(kind, row)
                scale = water * (helm.get(kind, row) + around) + (1.0 - water)
                inverse = 0.8 / scale
                start = inverse * rhs.get(kind, row)
                diag.put(kind, row, scale)
                base.put(kind, row, start)
                gain.put(kind, row, inverse * water)
                flow.put(kind, row, water * start)

    rows_loop(0, BLOCK, 4, smooth_setup)
    flow.wrap()

    def smooth_second(i, count):
        for group in near_rows(flow, i, count, 1):
            for kind, row, near in group:
                value = 1.2 * base.get(kind, row) + gain.get(kind, row) * near
                state.put(kind, row, value)
                flow_next.put(kind, row, wet.get(kind, row) * value)

    rows_loop(0, BLOCK, 8, smooth_second)
    flow_next.wrap()

    def pair_sum(value):
        value = value + jnp.where(
            level % 2 == 0, pltpu.roll(value, CZ - 1, 0), pltpu.roll(value, 1, 0)
        )
        return value + jnp.where(
            lane % 2 == 0, pltpu.roll(value, LANES - 1, 1), pltpu.roll(value, 1, 1)
        )

    def coarse_mask(j, count):
        for k in range(count):
            for kind, row in cells(j + k, ALL, BLOCK // 2):
                total = pair_sum(wet.get(kind, 2 * row) + wet.get(kind, 2 * row + 1))
                wet_c.put(kind, row, jnp.where(total >= 3.5, 1.0, 0.0))

    rows_loop(0, BLOCK // 2, 4, coarse_mask)
    wet_c.wrap()

    low, high = eig_ref[0], eig_ref[1]
    centre = 0.5 * (high + low)
    half = 0.5 * (high - low)
    sigma = centre / half
    rho = 1.0 / sigma
    start_scale = 1.0 / centre

    def coarse_setup(j, count):
        fine_near = near_rows(flow_next, 2 * j, 2 * count, 1)
        for group in near_rows(wet_c, j, count, 2):
            sources, shifts = [0.0] * len(group), [0.0] * len(group)
            for _ in range(2):
                for n, (kind, row, near) in enumerate(next(fine_near)):
                    left_over = rhs.get(kind, row) - diag.get(kind, row) * state.get(kind, row)
                    sources[n] = sources[n] + wet.get(kind, row) * (left_over + near)
                    shifts[n] = shifts[n] + helm.get(kind, row)
            for n, (kind, row, count_c) in enumerate(group):
                source, shift = 0.125 * pair_sum(sources[n]), 0.125 * pair_sum(shifts[n])
                water_c = wet_c.get(kind, row)
                scale = water_c * (shift + 0.25 * count_c) + (1.0 - water_c)
                inverse = 1.0 / scale
                first = source * inverse * start_scale
                diag_c.put(kind, row, scale)
                inverse_c.put(kind, row, inverse)
                remain.put(kind, row, source)
                error.put(kind, row, first)
                spread.put(kind, row, first)
                masked.put(kind, row, water_c * first)

    rows_loop(0, BLOCK // 2, 2, coarse_setup)
    masked.wrap()

    direction, now, later = spread, masked, masked_next
    for sweep in range(1, CHEB):
        rho_next = 1.0 / (2.0 * sigma - rho)
        keep = rho_next * rho
        add = 2.0 * rho_next / half

        def chebyshev(j, count, sweep=sweep, keep=keep, add=add, now=now, later=later):
            for group in near_rows(now, j, count, 2):
                for kind, row, near in group:
                    old = direction.get(kind, row)
                    water_c = wet_c.get(kind, row)
                    image = diag_c.get(kind, row) * old - 0.25 * water_c * near
                    left_over = remain.get(kind, row) - image
                    fresh = keep * old + add * (left_over * inverse_c.get(kind, row))
                    error.put(kind, row, error.get(kind, row) + fresh)
                    if sweep + 1 < CHEB:
                        remain.put(kind, row, left_over)
                        direction.put(kind, row, fresh)
                        later.put(kind, row, water_c * fresh)

        rows_loop(0, BLOCK // 2, 8, chebyshev)
        if sweep + 1 < CHEB:
            later.wrap()
        rho = rho_next
        now, later = later, now

    def prolong(j, count):
        for k in range(count):
            group = cells(j + k, ALL, BLOCK // 2)
            values = [error.get(*cell) for cell in group]
            sides = beside(list(zip(ALL, values)), values[-1], 1)
            for value, pair, cell in zip(values, sides, group):
                line = 0.75 * value + 0.25 * jnp.where(lane % 2 == 0, *pair)
                other = jnp.where(
                    level % 2 == 0, pltpu.roll(line, 1, 0), pltpu.roll(line, CZ - 1, 0)
                )
                other = jnp.where((level == 0) | (level == CZ - 1), 0.0, other)
                spread.put(*cell, 0.75 * line + 0.25 * other)

    rows_loop(0, BLOCK // 2, 4, prolong)
    spread.wrap()

    def correct(chosen):
        def step(j, count):
            for k in range(count):
                for kind, row in cells(j + k, chosen, BLOCK // 2):
                    here = 0.75 * spread.get(kind, row)
                    for fine, beyond in ((2 * row, row - 1), (2 * row + 1, row + 1)):
                        water = wet.get(kind, fine)
                        value = here + 0.25 * spread.get(kind, beyond)
                        value = state.get(kind, fine) + water * value
                        state.put(kind, fine, value)
                        flow.put(kind, fine, water * value)

        return step

    rows_loop(0, 5, 5, correct((1, 2, 3)))
    rows_loop(5, BLOCK // 2, 3, correct((0, 1, 2)))
    flow.wrap()

    for now, later in ((flow, flow_next), (flow_next, flow)):

        def smooth(chosen, now=now, later=later):
            def step(i, count):
                for group in near_rows(now, i, count, 1, chosen):
                    for kind, row, near in group:
                        value = 0.2 * state.get(kind, row) + base.get(kind, row)
                        value = value + gain.get(kind, row) * near
                        state.put(kind, row, value)
                        later.put(kind, row, wet.get(kind, row) * value)

            return step

        rows_loop(0, 12, 6, smooth((1, 2)))
        rows_loop(12, BLOCK, 4, smooth((0, 1, 2)))
        later.wrap()

    def finish(chosen):
        def step(i, count):
            for group in near_rows(flow, i, count, 1, chosen):
                for kind, row, near in group[:-1]:
                    value = state.get(0, row)
                    left_over = rhs.get(0, row) - diag.get(0, row) * value
                    left_over = left_over + wet.get(0, row) * near
                    pressure_ref[pl.ds(row - RIM, CZ, stride=ROWS), :] = value
                    residual_ref[pl.ds(row - RIM, CZ, stride=ROWS), :] = left_over

        return step

    rows_loop(0, RIM, 7, finish((1, 2)))
    rows_loop(RIM, BLOCK, 2, finish((0, 1)))
    copies = (
        pltpu.make_async_copy(pressure_ref, pressure_out, out_sem.at[0]),
        pltpu.make_async_copy(residual_ref, residual_out, out_sem.at[1]),
    )
    for copy in copies:
        copy.start()
    for copy in copies:
        copy.wait()


def swapped(array, axis, first):
    pairs = [(i, i + 1) for i in range(first, lax.axis_size(axis) - 1, 2)]
    return lax.ppermute(array, axis, pairs + [(j, i) for i, j in pairs])


def in_hbm(array):
    return pltpu.with_memory_space_constraint(array, pltpu.HBM)


def f32(*shape):
    return jax.ShapeDtypeStruct(shape, jnp.float32)


def body(right_side, wet_mask, helmholtz, eig_low, eig_high):
    flat = (CZ * ROWS, LANES)
    right_flat = right_side.reshape(flat)
    mask_flat = wet_mask.reshape(flat)
    helm_flat = helmholtz.reshape(flat)
    limits = pltpu.CompilerParams(vmem_limit_bytes=24 * 1024 * 1024)

    far, near, own = pl.pallas_call(
        strips_kernel,
        out_shape=(f32(STRIP, CZ, LANES), f32(STRIP, CZ, LANES), f32(3, ROWS, CZ, LANES)),
        in_specs=[HBM] * 3,
        out_specs=(VMEM,) * 3,
        scratch_shapes=[
            pltpu.VMEM(flat, jnp.int32),
            pltpu.VMEM(flat, jnp.float32),
            pltpu.VMEM(flat, jnp.float32),
            pltpu.SemaphoreType.DMA((3,)),
        ],
        compiler_params=limits,
        name="strips",
    )(in_hbm(right_flat), in_hbm(mask_flat), in_hbm(helm_flat))
    far = swapped(far, "wide", 1)
    near = swapped(near, "wide", 0)

    tall, far, near, eigs = pl.pallas_call(
        sides_kernel,
        out_shape=(
            f32(3, TALL, CZ, LANES),
            f32(3 * PACKED, CZ, LANES),
            f32(3 * PACKED, CZ, LANES),
            f32(2, CZ, LANES),
        ),
        in_specs=[SMEM] * 2 + [VMEM] * 3,
        out_specs=(VMEM,) * 4,
        compiler_params=limits,
        name="sides",
    )(eig_low, eig_high, own, far, near)
    far = swapped(far, "narrow", 1)
    near = swapped(near, "narrow", 0)

    padded = [((rows + 3) * PITCH, LANES) for rows in (TALL, BLOCK)]
    plain = [(rows + 2, CZ, LANES) for rows in (TALL, BLOCK)]
    padded_c = [((rows // 2 + 3) * PITCH, LANES) for rows in (TALL, BLOCK)]
    plain_c = [(rows // 2 + 2, CZ, LANES) for rows in (TALL, BLOCK)]
    shapes = padded * 3 + plain * 4 + padded_c * 3 + plain_c * 5 + [plain[1]] * 2 + [flat] * 2
    pressure, residual = pl.pallas_call(
        cycle_kernel,
        out_shape=(f32(*flat),) * 2,
        in_specs=[VMEM] * 4,
        out_specs=(HBM,) * 2,
        scratch_shapes=[pltpu.VMEM(shape, jnp.float32) for shape in shapes]
        + [pltpu.SemaphoreType.DMA((2,))],
        compiler_params=limits,
        name="cycle",
    )(eigs, tall, far, near)
    shape = (CZ, ROWS, LANES)
    return pressure.reshape(shape), residual.reshape(shape)


def solution(mesh):
    field = P(None, "wide", "narrow")
    return jax.shard_map(
        body,
        mesh=mesh,
        in_specs=(field, field, field, P(), P()),
        out_specs=(field, field),
        check_vma=False,
    )
```

```python
import functools

import jax
import jax.numpy as jnp
from jax import lax
from jax.experimental import pallas as pl
from jax.experimental.pallas import tpu as pltpu
from jax.sharding import PartitionSpec as P

CHEB = 4

CZ = 8
ROWS = 32
LANES = 128
RIM = 14
TALL = ROWS + 2 * RIM + 4
MASK_RIM = 13
RIGHT_RIM = 12
STRIP = MASK_RIM + 2 * RIGHT_RIM
SIDE = 16
SPAN = 2 * SIDE
BLOCK = TALL * SPAN // LANES
BLOCKS = LANES // SPAN
ALL = tuple(range(BLOCKS))
PACKED = BLOCK // 2
PITCH = 2 * CZ

VMEM = pl.BlockSpec(memory_space=pltpu.VMEM)
SMEM = pl.BlockSpec(memory_space=pltpu.SMEM)
HBM = pl.BlockSpec(memory_space=pltpu.HBM)


def brick_row(ref, row):
    return ref[pl.ds(row, CZ, stride=ROWS), :]


def strips_kernel(
    right_hbm, mask_hbm, helm_hbm, far_ref, near_ref, own_ref, mask_ref, helm_ref, right_ref, sem
):
    odd = lax.rem(lax.axis_index("wide"), 2)
    copies = [
        pltpu.make_async_copy(source, dest, sem.at[k])
        for k, (source, dest) in enumerate(
            ((mask_hbm, mask_ref), (helm_hbm, helm_ref), (right_hbm, right_ref))
        )
    ]
    for copy in copies:
        copy.start()
    for field, (ref, rim, offset) in enumerate(
        (
            (mask_ref, MASK_RIM, 0),
            (helm_ref, RIGHT_RIM, MASK_RIM),
            (right_ref, RIGHT_RIM, MASK_RIM + RIGHT_RIM),
        )
    ):
        copies[field].wait()
        for row in range(ROWS):
            line = brick_row(ref, row).astype(jnp.float32)
            own_ref[field, row] = line
        to_far, to_near = (ROWS - rim) * odd, (ROWS - rim) * (1 - odd)
        for row in range(rim):
            far_ref[offset + row] = own_ref[field, to_far + row]
            near_ref[offset + row] = own_ref[field, to_near + row]


def sides_kernel(
    low_ref, high_ref, own_ref, far_ref, near_ref, tall_ref, far_out, near_out, eig_ref
):
    odd = lax.rem(lax.axis_index("wide"), 2)
    odd_column = lax.rem(lax.axis_index("narrow"), 2) == 1
    eig_ref[0] = jnp.full((CZ, LANES), low_ref[0], jnp.float32)
    eig_ref[1] = jnp.full((CZ, LANES), high_ref[0], jnp.float32)
    zero = jnp.zeros((CZ, LANES), jnp.float32)
    lane = lax.broadcasted_iota(jnp.int32, (CZ, LANES), 1)
    for field, offset, rim in (
        (0, 0, MASK_RIM),
        (1, MASK_RIM, RIGHT_RIM),
        (2, MASK_RIM + RIGHT_RIM, RIGHT_RIM),
    ):
        for row in (0, 1) + tuple(range(TALL - 6, TALL)):
            tall_ref[field, row] = zero
        from_far = RIM - rim + (ROWS + rim) * odd
        from_near = RIM - rim + (ROWS + rim) * (1 - odd)
        for row in range(rim):
            tall_ref[field, from_far + row] = far_ref[offset + row]
            tall_ref[field, from_near + row] = near_ref[offset + row]
        for row in range(ROWS):
            tall_ref[field, RIM + row] = own_ref[field, row]

    block, half = lane // SPAN, lane & (SPAN - 1) < SIDE

    def pack(start, count):
        for i, field in ((start + k, field) for k in range(count) for field in range(3)):
            first, last = zero, zero
            for b in range(BLOCKS):
                low = tall_ref[field, BLOCK * b + i]
                low = pltpu.roll(low, SPAN * b + SIDE, 1)
                high = tall_ref[field, BLOCK * b + i + BLOCK // 2]
                high = pltpu.roll(high, SPAN * (b + 1), 1) if b + 1 < BLOCKS else high
                here, after = block == b, block == (b + 1) % BLOCKS
                last = jnp.where(here, jnp.where(half, low, high), last)
                first = jnp.where(here & ~half, low, jnp.where(after & half, high, first))
            place = field * PACKED + i
            far_out[place] = jnp.where(odd_column, last, first)
            near_out[place] = jnp.where(odd_column, first, last)

    rows_loop(0, PACKED, 4, pack)


def rows_loop(start, stop, chunk, step):
    count = (stop - start) // chunk
    assert count * chunk == stop - start
    if count == 1:
        step(start, chunk)
        return

    def body(index, carry):
        step(start + index * chunk, chunk)
        return carry

    lax.fori_loop(0, count, body, 0)


class Field:
    def __init__(self, main, side, height, ahead=(1, 1)):
        self.refs, self.height, self.ahead = (main, side), height, ahead

    def get(self, kind, row, shift=0):
        return self.refs[kind][row + self.ahead[kind]]

    def put(self, kind, row, value):
        self.refs[kind][row + self.ahead[kind]] = value

    def wrap(self):
        self.put(1, -1, pltpu.roll(self.get(1, self.height - 1), SPAN, 1))
        self.put(1, self.height, pltpu.roll(self.get(1, 0), LANES - SPAN, 1))


class Padded(Field):
    def get(self, kind, row, shift=0):
        return self.refs[kind][pl.ds(row * PITCH + (PITCH + CZ + shift), CZ), :]

    def put(self, kind, row, value):
        self.refs[kind][pl.ds(row * PITCH + (PITCH + CZ), CZ), :] = value

    def clear(self, reach):
        zero = jnp.zeros((CZ, LANES), jnp.float32)
        for ref, count in zip(self.refs, (self.height * BLOCKS, self.height)):
            for place in [CZ - 1 - k for k in range(reach)] + [2 * CZ + k for k in range(reach)]:
                for first in range(0, count, CZ):
                    ref[pl.ds((first + 1) * PITCH + place, CZ, stride=PITCH), :] = zero


def cycle_kernel(eig_ref, tall_ref, far_ref, near_ref, pressure_out, residual_out, *scratch):
    scratch = list(scratch)
    out_sem = scratch.pop()
    residual_ref, pressure_ref = scratch.pop(), scratch.pop()

    def fields(kind, height, count):
        return [kind(scratch.pop(0), scratch.pop(0), height) for _ in range(count)]

    wet, flow, flow_next = fields(Padded, BLOCK, 3)
    diag, base, gain, state = fields(Field, BLOCK, 4)
    wet_c, masked, masked_next = fields(Padded, BLOCK // 2, 3)
    diag_c, inverse_c, remain, error, spread = fields(Field, BLOCK // 2, 5)
    helm = Field(tall_ref.at[1], scratch.pop(0), BLOCK, (0, 1))
    rhs = Field(tall_ref.at[2], scratch.pop(0), BLOCK, (0, 1))

    lane = lax.broadcasted_iota(jnp.int32, (CZ, LANES), 1)
    level = lax.broadcasted_iota(jnp.int32, (CZ, LANES), 0)
    place = lane & (SPAN - 1)
    spots = {1: place, 2: lax.shift_right_logical(place, 1)}

    wet.clear(1)
    flow.clear(1)
    flow_next.clear(1)
    wet_c.clear(2)
    masked.clear(2)
    masked_next.clear(2)

    odd_column = lax.rem(lax.axis_index("narrow"), 2) == 1

    def copy_wet(row, count):
        for k in range(count):
            wet.put(0, row + k, tall_ref[0, row + k])

    rows_loop(0, TALL, 16, copy_wet)

    def unpack(i, count):
        for k in range(count):
            for index, field in enumerate((wet, helm, rhs)):
                far, near = far_ref[index * PACKED + i + k], near_ref[index * PACKED + i + k]
                right = jnp.where(odd_column, far, near)
                left = jnp.where(odd_column, near, far)
                field.put(1, i + k, jnp.where(place < SIDE, left, right))
                late = jnp.where(place < SIDE, right, left)
                field.put(1, i + k + PACKED, pltpu.roll(late, LANES - SIDE, 1))

    rows_loop(0, PACKED, 4, unpack)
    wet.wrap()

    def cells(i, chosen, height):
        return [(0, height * b + i) for b in chosen] + [(1, i)]

    def beside(mains, side, reach):
        edge = side
        found = []
        for b, main in mains:
            inner = pltpu.roll(side, (LANES - SIDE - SPAN * b) % LANES, 1)
            before = jnp.where(lane >= LANES - reach, inner, main)
            after = jnp.where(lane < reach, inner, main)
            found.append((pltpu.roll(before, reach, 1), pltpu.roll(after, LANES - reach, 1)))
            other = pltpu.roll(main, SIDE + SPAN * b, 1)
            edge = jnp.where(lane >= SPAN * b, other, edge) if b else other
        before = jnp.where(spots[reach] == SIDE // reach - 1, edge, side)
        after = jnp.where(spots[reach] == SIDE // reach, edge, side)
        found.append((pltpu.roll(before, reach, 1), pltpu.roll(after, LANES - reach, 1)))
        return found

    def near_rows(field, i, count, reach, chosen=ALL):
        lines = [[field.get(*cell) for cell in cells(i + k, chosen, field.height)] for k in (-1, 0)]
        for k in range(count):
            lines.append([field.get(*cell) for cell in cells(i + k + 1, chosen, field.height)])
            here = lines[k + 1]
            sides = beside(list(zip(chosen, here)), here[-1], reach)
            out = []
            for n, (kind, row) in enumerate(cells(i + k, chosen, field.height)):
                total = lines[k][n] + lines[k + 2][n]
                total = total + (field.get(kind, row, -reach) + field.get(kind, row, reach))
                out.append((kind, row, total + (sides[n][0] + sides[n][1])))
            yield out

    def smooth_setup(i, count):
        for group in near_rows(wet, i, count, 1):
            for kind, row, around in group:
                water = wet.get(kind, row)
                scale = water * (helm.get(kind, row) + around) + (1.0 - water)
                inverse = 0.8 / scale
                start = inverse * rhs.get(kind, row)
                diag.put(kind, row, scale)
                base.put(kind, row, start)
                gain.put(kind, row, inverse * water)
                flow.put(kind, row, water * start)

    rows_loop(0, BLOCK, 4, smooth_setup)
    flow.wrap()

    def smooth_second(i, count):
        for group in near_rows(flow, i, count, 1):
            for kind, row, near in group:
                value = 1.2 * base.get(kind, row) + gain.get(kind, row) * near
                state.put(kind, row, value)
                flow_next.put(kind, row, wet.get(kind, row) * value)

    rows_loop(0, BLOCK, 4, smooth_second)
    flow_next.wrap()

    def pair_sum(value):
        value = value + jnp.where(
            level & 1 == 0, pltpu.roll(value, CZ - 1, 0), pltpu.roll(value, 1, 0)
        )
        return value + jnp.where(
            lane & 1 == 0, pltpu.roll(value, LANES - 1, 1), pltpu.roll(value, 1, 1)
        )

    def coarse_mask(j, count):
        for k in range(count):
            for kind, row in cells(j + k, ALL, BLOCK // 2):
                total = pair_sum(wet.get(kind, 2 * row) + wet.get(kind, 2 * row + 1))
                wet_c.put(kind, row, jnp.where(total >= 3.5, 1.0, 0.0))

    rows_loop(0, BLOCK // 2, 4, coarse_mask)
    wet_c.wrap()

    low, high = eig_ref[0], eig_ref[1]
    centre = 0.5 * (high + low)
    half = 0.5 * (high - low)
    sigma = centre / half
    rho = 1.0 / sigma
    start_scale = 1.0 / centre

    def coarse_setup(j, count):
        fine_near = near_rows(flow_next, 2 * j, 2 * count, 1)
        for group in near_rows(wet_c, j, count, 2):
            sources, shifts = [0.0] * len(group), [0.0] * len(group)
            for _ in range(2):
                for n, (kind, row, near) in enumerate(next(fine_near)):
                    left_over = rhs.get(kind, row) - diag.get(kind, row) * state.get(kind, row)
                    sources[n] = sources[n] + wet.get(kind, row) * (left_over + near)
                    shifts[n] = shifts[n] + helm.get(kind, row)
            for n, (kind, row, count_c) in enumerate(group):
                source, shift = 0.125 * pair_sum(sources[n]), 0.125 * pair_sum(shifts[n])
                water_c = wet_c.get(kind, row)
                scale = water_c * (shift + 0.25 * count_c) + (1.0 - water_c)
                inverse = 1.0 / scale
                first = source * inverse * start_scale
                diag_c.put(kind, row, scale)
                inverse_c.put(kind, row, inverse)
                remain.put(kind, row, source)
                error.put(kind, row, first)
                spread.put(kind, row, first)
                masked.put(kind, row, water_c * first)

    rows_loop(0, BLOCK // 2, 2, coarse_setup)
    masked.wrap()

    direction, now, later = spread, masked, masked_next
    for sweep in range(1, CHEB):
        rho_next = 1.0 / (2.0 * sigma - rho)
        keep = rho_next * rho
        add = 2.0 * rho_next / half

        def chebyshev(j, count, sweep=sweep, keep=keep, add=add, now=now, later=later):
            for group in near_rows(now, j, count, 2):
                for kind, row, near in group:
                    old = direction.get(kind, row)
                    water_c = wet_c.get(kind, row)
                    image = diag_c.get(kind, row) * old - 0.25 * water_c * near
                    left_over = remain.get(kind, row) - image
                    fresh = keep * old + add * (left_over * inverse_c.get(kind, row))
                    error.put(kind, row, error.get(kind, row) + fresh)
                    if sweep + 1 < CHEB:
                        remain.put(kind, row, left_over)
                        direction.put(kind, row, fresh)
                        later.put(kind, row, water_c * fresh)

        rows_loop(0, BLOCK // 2, 4, chebyshev)
        if sweep + 1 < CHEB:
            later.wrap()
        rho = rho_next
        now, later = later, now

    def prolong(j, count):
        for k in range(count):
            group = cells(j + k, ALL, BLOCK // 2)
            values = [error.get(*cell) for cell in group]
            sides = beside(list(zip(ALL, values)), values[-1], 1)
            for value, pair, cell in zip(values, sides, group):
                line = 0.75 * value + 0.25 * jnp.where(lane & 1 == 0, *pair)
                other = jnp.where(
                    level & 1 == 0, pltpu.roll(line, 1, 0), pltpu.roll(line, CZ - 1, 0)
                )
                other = jnp.where((level == 0) | (level == CZ - 1), 0.0, other)
                spread.put(*cell, 0.75 * line + 0.25 * other)

    rows_loop(0, BLOCK // 2, 4, prolong)
    spread.wrap()

    def correct(chosen):
        def step(j, count):
            for k in range(count):
                for kind, row in cells(j + k, chosen, BLOCK // 2):
                    here = 0.75 * spread.get(kind, row)
                    for fine, beyond in ((2 * row, row - 1), (2 * row + 1, row + 1)):
                        water = wet.get(kind, fine)
                        value = here + 0.25 * spread.get(kind, beyond)
                        value = state.get(kind, fine) + water * value
                        state.put(kind, fine, value)
                        flow.put(kind, fine, water * value)

        return step

    rows_loop(0, 5, 5, correct((1, 2, 3)))
    rows_loop(5, BLOCK // 2, 3, correct((0, 1, 2)))
    flow.wrap()

    for now, later in ((flow, flow_next), (flow_next, flow)):

        def smooth(chosen, now=now, later=later):
            def step(i, count):
                for group in near_rows(now, i, count, 1, chosen):
                    for kind, row, near in group:
                        value = 0.2 * state.get(kind, row) + base.get(kind, row)
                        value = value + gain.get(kind, row) * near
                        state.put(kind, row, value)
                        later.put(kind, row, wet.get(kind, row) * value)

            return step

        rows_loop(0, 12, 6, smooth((1, 2)))
        rows_loop(12, BLOCK, 4, smooth((0, 1, 2)))
        later.wrap()

    def finish(chosen):
        def step(i, count):
            for group in near_rows(flow, i, count, 1, chosen):
                for kind, row, near in group[:-1]:
                    value = state.get(0, row)
                    left_over = rhs.get(0, row) - diag.get(0, row) * value
                    left_over = left_over + wet.get(0, row) * near
                    pressure_ref[pl.ds(row - RIM, CZ, stride=ROWS), :] = value
                    residual_ref[pl.ds(row - RIM, CZ, stride=ROWS), :] = left_over

        return step

    rows_loop(0, RIM, 7, finish((1, 2)))
    rows_loop(RIM, BLOCK, 2, finish((0, 1)))
    copies = (
        pltpu.make_async_copy(pressure_ref, pressure_out, out_sem.at[0]),
        pltpu.make_async_copy(residual_ref, residual_out, out_sem.at[1]),
    )
    for copy in copies:
        copy.start()
    for copy in copies:
        copy.wait()


def swapped(array, axis, first):
    pairs = [(i, i + 1) for i in range(first, lax.axis_size(axis) - 1, 2)]
    return lax.ppermute(array, axis, pairs + [(j, i) for i, j in pairs])


def in_hbm(array):
    return pltpu.with_memory_space_constraint(array, pltpu.HBM)


def f32(*shape):
    return jax.ShapeDtypeStruct(shape, jnp.float32)


def body(right_side, wet_mask, helmholtz, eig_low, eig_high):
    flat = (CZ * ROWS, LANES)
    right_flat = right_side.reshape(flat)
    mask_flat = wet_mask.reshape(flat)
    helm_flat = helmholtz.reshape(flat)
    limits = pltpu.CompilerParams(vmem_limit_bytes=24 * 1024 * 1024)

    far, near, own = pl.pallas_call(
        strips_kernel,
        out_shape=(f32(STRIP, CZ, LANES), f32(STRIP, CZ, LANES), f32(3, ROWS, CZ, LANES)),
        in_specs=[HBM] * 3,
        out_specs=(VMEM,) * 3,
        scratch_shapes=[
            pltpu.VMEM(flat, jnp.int32),
            pltpu.VMEM(flat, jnp.float32),
            pltpu.VMEM(flat, jnp.float32),
            pltpu.SemaphoreType.DMA((3,)),
        ],
        compiler_params=limits,
        name="strips",
    )(in_hbm(right_flat), in_hbm(mask_flat), in_hbm(helm_flat))
    far = swapped(far, "wide", 1)
    near = swapped(near, "wide", 0)

    tall, far, near, eigs = pl.pallas_call(
        sides_kernel,
        out_shape=(
            f32(3, TALL, CZ, LANES),
            f32(3 * PACKED, CZ, LANES),
            f32(3 * PACKED, CZ, LANES),
            f32(2, CZ, LANES),
        ),
        in_specs=[SMEM] * 2 + [VMEM] * 3,
        out_specs=(VMEM,) * 4,
        compiler_params=limits,
        name="sides",
    )(eig_low, eig_high, own, far, near)
    far = swapped(far, "narrow", 1)
    near = swapped(near, "narrow", 0)

    padded = [((rows + 3) * PITCH, LANES) for rows in (TALL, BLOCK)]
    plain = [(rows + 2, CZ, LANES) for rows in (TALL, BLOCK)]
    padded_c = [((rows // 2 + 3) * PITCH, LANES) for rows in (TALL, BLOCK)]
    plain_c = [(rows // 2 + 2, CZ, LANES) for rows in (TALL, BLOCK)]
    shapes = padded * 3 + plain * 4 + padded_c * 3 + plain_c * 5 + [plain[1]] * 2 + [flat] * 2
    pressure, residual = pl.pallas_call(
        cycle_kernel,
        out_shape=(f32(*flat),) * 2,
        in_specs=[VMEM] * 4,
        out_specs=(HBM,) * 2,
        scratch_shapes=[pltpu.VMEM(shape, jnp.float32) for shape in shapes]
        + [pltpu.SemaphoreType.DMA((2,))],
        compiler_params=limits,
        name="cycle",
    )(eigs, tall, far, near)
    shape = (CZ, ROWS, LANES)
    return pressure.reshape(shape), residual.reshape(shape)


def solution(mesh):
    field = P(None, "wide", "narrow")
    return jax.shard_map(
        body,
        mesh=mesh,
        in_specs=(field, field, field, P(), P()),
        out_specs=(field, field),
        check_vma=False,
    )
```

```python
import functools

import jax
import jax.numpy as jnp
from jax import lax
from jax.experimental import pallas as pl
from jax.experimental.pallas import tpu as pltpu
from jax.sharding import PartitionSpec as P

CHEB = 4

CZ = 8
ROWS = 32
LANES = 128
RIM = 14
TALL = ROWS + 2 * RIM + 4
MASK_RIM = 13
RIGHT_RIM = 12
STRIP = MASK_RIM + 2 * RIGHT_RIM
SIDE = 16
SPAN = 2 * SIDE
BLOCK = TALL * SPAN // LANES
BLOCKS = LANES // SPAN
PACKED = BLOCK // 2
PITCH = 2 * CZ

VMEM = pl.BlockSpec(memory_space=pltpu.VMEM)
SMEM = pl.BlockSpec(memory_space=pltpu.SMEM)
HBM = pl.BlockSpec(memory_space=pltpu.HBM)


def brick_row(ref, row):
    return ref[pl.ds(row, CZ, stride=ROWS), :]


def strips_kernel(
    right_hbm, mask_hbm, helm_hbm, far_ref, near_ref, own_ref, mask_ref, helm_ref, right_ref, sem
):
    odd = lax.rem(lax.axis_index("wide"), 2)
    copies = [
        pltpu.make_async_copy(source, dest, sem.at[k])
        for k, (source, dest) in enumerate(
            ((mask_hbm, mask_ref), (helm_hbm, helm_ref), (right_hbm, right_ref))
        )
    ]
    for copy in copies:
        copy.start()
    for field, (ref, rim, offset) in enumerate(
        (
            (mask_ref, MASK_RIM, 0),
            (helm_ref, RIGHT_RIM, MASK_RIM),
            (right_ref, RIGHT_RIM, MASK_RIM + RIGHT_RIM),
        )
    ):
        copies[field].wait()
        for row in range(ROWS):
            line = brick_row(ref, row).astype(jnp.float32)
            own_ref[field, row] = line
        to_far, to_near = (ROWS - rim) * odd, (ROWS - rim) * (1 - odd)
        for row in range(rim):
            far_ref[offset + row] = own_ref[field, to_far + row]
            near_ref[offset + row] = own_ref[field, to_near + row]


def sides_kernel(
    low_ref, high_ref, own_ref, far_ref, near_ref, tall_ref, far_out, near_out, eig_ref
):
    odd = lax.rem(lax.axis_index("wide"), 2)
    odd_column = lax.rem(lax.axis_index("narrow"), 2) == 1
    eig_ref[0] = jnp.full((CZ, LANES), low_ref[0], jnp.float32)
    eig_ref[1] = jnp.full((CZ, LANES), high_ref[0], jnp.float32)
    zero = jnp.zeros((CZ, LANES), jnp.float32)
    lane = lax.broadcasted_iota(jnp.int32, (CZ, LANES), 1)
    for field, offset, rim in (
        (0, 0, MASK_RIM),
        (1, MASK_RIM, RIGHT_RIM),
        (2, MASK_RIM + RIGHT_RIM, RIGHT_RIM),
    ):
        for row in (0, 1) + tuple(range(TALL - 6, TALL)):
            tall_ref[field, row] = zero
        from_far = RIM - rim + (ROWS + rim) * odd
        from_near = RIM - rim + (ROWS + rim) * (1 - odd)
        for row in range(rim):
            tall_ref[field, from_far + row] = far_ref[offset + row]
            tall_ref[field, from_near + row] = near_ref[offset + row]
        for row in range(ROWS):
            tall_ref[field, RIM + row] = own_ref[field, row]

    block, half = lane // SPAN, lane & (SPAN - 1) < SIDE

    def pack(start, count):
        for i, field in ((start + k, field) for k in range(count) for field in range(3)):
            first, last = zero, zero
            for b in range(BLOCKS):
                low = tall_ref[field, BLOCK * b + i]
                low = pltpu.roll(low, SPAN * b + SIDE, 1)
                high = tall_ref[field, BLOCK * b + i + BLOCK // 2]
                high = pltpu.roll(high, SPAN * (b + 1), 1) if b + 1 < BLOCKS else high
                here, after = block == b, block == (b + 1) % BLOCKS
                last = jnp.where(here, jnp.where(half, low, high), last)
                first = jnp.where(here & ~half, low, jnp.where(after & half, high, first))
            place = field * PACKED + i
            far_out[place] = jnp.where(odd_column, last, first)
            near_out[place] = jnp.where(odd_column, first, last)

    rows_loop(0, PACKED, 4, pack)


def rows_loop(start, stop, chunk, step):
    count = (stop - start) // chunk
    assert count * chunk == stop - start

    if count == 1:
        step(start, chunk)
        return

    def body(index, carry):
        step(start + index * chunk, chunk)
        return carry

    lax.fori_loop(0, count, body, 0)


def cycle_kernel(
    eig_ref,
    tall_ref,
    far_ref,
    near_ref,
    pressure_out,
    residual_out,
    wet,
    flow,
    flow_next,
    helm_side,
    rhs_side,
    diag,
    base,
    gain,
    state,
    wet_c,
    masked,
    masked_next,
    diag_c,
    inverse_c,
    remain,
    error,
    direction,
    pressure_ref,
    residual_ref,
    out_sem,
):
    lane = lax.broadcasted_iota(jnp.int32, (CZ, LANES), 1)
    level = lax.broadcasted_iota(jnp.int32, (CZ, LANES), 0)
    zero = jnp.zeros((CZ, LANES), jnp.float32)
    tiles = (0, 1)

    def put(ref, tile, row, value):
        ref[tile, pl.ds(row * PITCH + CZ, CZ), :] = value

    def get(ref, tile, row, shift=0):
        return ref[tile, pl.ds(row * PITCH + (CZ + shift), CZ), :]

    def clear(ref, count, reach):
        for place in [CZ - 1 - k for k in range(reach)] + [2 * CZ + k for k in range(reach)]:
            for first in range(0, count, CZ):
                first = min(first, count - CZ)
                for tile in tiles:
                    ref[tile, pl.ds(first * PITCH + place, CZ, stride=PITCH), :] = zero

    for ref in (wet, flow, flow_next):
        clear(ref, TALL, 1)
    for ref in (wet_c, masked, masked_next):
        clear(ref, TALL // 2, 2)

    def beside(main, side, reach):
        low, high = lane < reach, lane >= LANES - reach
        main_up, side_up = pltpu.roll(main, reach, 1), pltpu.roll(side, reach, 1)
        main_down = pltpu.roll(main, LANES - reach, 1)
        side_down = pltpu.roll(side, LANES - reach, 1)
        return (
            (jnp.where(low, side_up, main_up), jnp.where(high, side_down, main_down)),
            (jnp.where(low, main_up, side_up), jnp.where(high, main_down, side_down)),
        )

    def near_rows(ref, row, count, reach):
        lines = [[get(ref, tile, row + k - 1) for tile in tiles] for k in range(2)]
        for k in range(count):
            lines.append([get(ref, tile, row + k + 1) for tile in tiles])
            here = lines[k + 1]
            sides = beside(here[0], here[1], reach)
            yield [
                (lines[k][tile] + lines[k + 2][tile])
                + (get(ref, tile, row + k, -reach) + get(ref, tile, row + k, reach))
                + (sides[tile][0] + sides[tile][1])
                for tile in tiles
            ]

    odd_column = lax.rem(lax.axis_index("narrow"), 2) == 1

    def unpack(start, count):
        edges = (lane < SIDE) | (lane >= LANES - SIDE)
        left_half = lane & (SPAN - 1) < SIDE
        for i, field in ((start + k, field) for k in range(count) for field in range(3)):
            far, near = far_ref[field * PACKED + i], near_ref[field * PACKED + i]
            right = jnp.where(odd_column, far, near)
            left = jnp.where(odd_column, near, far)
            early = jnp.where(left_half, left, right)
            late = jnp.where(left_half, right, left)
            for b in range(BLOCKS):
                low = pltpu.roll(early, LANES - SPAN * b - SIDE, 1)
                high = pltpu.roll(late, LANES - SPAN * (b + 1), 1) if b + 1 < BLOCKS else late
                for row, side in ((BLOCK * b + i, low), (BLOCK * b + i + PACKED, high)):
                    side = jnp.where(edges, side, 0.0)
                    if field == 0:
                        put(wet, 0, row, tall_ref[0, row])
                        put(wet, 1, row, side)
                    else:
                        (helm_side, rhs_side)[field - 1][row] = side

    rows_loop(0, PACKED, 4, unpack)

    def helm(tile, row):
        return helm_side[row] if tile else tall_ref[1, row]

    def rhs(tile, row):
        return rhs_side[row] if tile else tall_ref[2, row]

    def smooth_setup(row, chunk):
        for k, count in enumerate(near_rows(wet, row, chunk, 1)):
            for tile in tiles:
                water = get(wet, tile, row + k)
                scale = water * (helm(tile, row + k) + count[tile]) + (1.0 - water)
                inverse = 0.8 / scale
                start = inverse * rhs(tile, row + k)
                diag[tile, row + k] = scale
                base[tile, row + k] = start
                gain[tile, row + k] = inverse * water
                put(flow, tile, row + k, water * start)

    rows_loop(2, 58, 28, smooth_setup)

    def smooth_second(row, chunk):
        for k, near in enumerate(near_rows(flow, row, chunk, 1)):
            for tile in tiles:
                value = 1.2 * base[tile, row + k] + gain[tile, row + k] * near[tile]
                state[tile, row + k] = value
                put(flow_next, tile, row + k, get(wet, tile, row + k) * value)

    rows_loop(3, 57, 27, smooth_second)

    def pair_sum(value):
        value = value + jnp.where(
            level % 2 == 0, pltpu.roll(value, CZ - 1, 0), pltpu.roll(value, 1, 0)
        )
        return value + jnp.where(
            lane % 2 == 0, pltpu.roll(value, LANES - 1, 1), pltpu.roll(value, 1, 1)
        )

    def coarse_mask(row, chunk):
        for k in range(chunk):
            for tile in tiles:
                fine = 2 * (row + k)
                total = pair_sum(get(wet, tile, fine) + get(wet, tile, fine + 1))
                put(wet_c, tile, row + k, jnp.where(total >= 3.5, 1.0, 0.0))

    rows_loop(1, 29, 28, coarse_mask)

    low, high = eig_ref[0], eig_ref[1]
    centre = 0.5 * (high + low)
    half = 0.5 * (high - low)
    sigma = centre / half
    rho = 1.0 / sigma
    start_scale = 1.0 / centre

    def coarse_setup(row, chunk):
        fine_near = near_rows(flow_next, 2 * row, 2 * chunk, 1)
        for k, count_c in enumerate(near_rows(wet_c, row, chunk, 2)):
            source, shift = [zero, zero], [zero, zero]
            for fine in (2 * (row + k), 2 * (row + k) + 1):
                near = next(fine_near)
                for tile in tiles:
                    left_over = rhs(tile, fine) - diag[tile, fine] * state[tile, fine]
                    source[tile] += get(wet, tile, fine) * (left_over + near[tile])
                    shift[tile] += helm(tile, fine)
            for tile in tiles:
                first_sum = 0.125 * pair_sum(source[tile])
                water_c = get(wet_c, tile, row + k)
                scale = water_c * (0.125 * pair_sum(shift[tile]) + 0.25 * count_c[tile])
                scale = scale + (1.0 - water_c)
                inverse = 1.0 / scale
                first = first_sum * inverse * start_scale
                diag_c[tile, row + k] = scale
                inverse_c[tile, row + k] = inverse
                remain[tile, row + k] = first_sum
                error[tile, row + k] = first
                direction[tile, row + k] = first
                put(masked, tile, row + k, water_c * first)

    rows_loop(2, 28, 13, coarse_setup)

    now, later = masked, masked_next
    for sweep in range(1, CHEB):
        rho_next = 1.0 / (2.0 * sigma - rho)
        keep = rho_next * rho
        add = 2.0 * rho_next / half

        def chebyshev(row, chunk, keep=keep, add=add, now=now, later=later):
            for k, near in enumerate(near_rows(now, row, chunk, 2)):
                for tile in tiles:
                    old = direction[tile, row + k]
                    water_c = get(wet_c, tile, row + k)
                    image = diag_c[tile, row + k] * old - 0.25 * water_c * near[tile]
                    left_over = remain[tile, row + k] - image
                    fresh = keep * old + add * (left_over * inverse_c[tile, row + k])
                    remain[tile, row + k] = left_over
                    direction[tile, row + k] = fresh
                    error[tile, row + k] = error[tile, row + k] + fresh
                    put(later, tile, row + k, water_c * fresh)

        rows_loop(2 + sweep, 28 - sweep, 26 - 2 * sweep, chebyshev)
        rho = rho_next
        now, later = later, now

    def spread(row, chunk):
        for k in range(chunk):
            value = [error[tile, row + k] for tile in tiles]
            sides = beside(value[0], value[1], 1)
            for tile in tiles:
                line = 0.75 * value[tile] + 0.25 * jnp.where(
                    lane % 2 == 0, sides[tile][0], sides[tile][1]
                )
                other = jnp.where(level % 2 == 0, pltpu.roll(line, 1, 0), pltpu.roll(line, CZ - 1, 0))
                other = jnp.where((level == 0) | (level == CZ - 1), 0.0, other)
                direction[tile, row + k] = 0.75 * line + 0.25 * other

    rows_loop(5, 25, 20, spread)

    def correct(row, chunk):
        for k in range(chunk):
            for tile in tiles:
                here = 0.75 * direction[tile, row + k]
                for fine, side in ((2 * (row + k), row + k - 1), (2 * (row + k) + 1, row + k + 1)):
                    water = get(wet, tile, fine)
                    value = state[tile, fine] + water * (here + 0.25 * direction[tile, side])
                    state[tile, fine] = value
                    put(flow, tile, fine, water * value)

    rows_loop(5, 25, 20, correct)

    def smooth(now, later, last=False):
        def step(row, chunk):
            for k, near in enumerate(near_rows(now, row, chunk, 1)):
                for tile in tiles:
                    value = 0.2 * state[tile, row + k] + base[tile, row + k]
                    value = value + gain[tile, row + k] * near[tile]
                    state[tile, row + k] = value
                    put(later, tile, row + k, get(wet, tile, row + k) * value)
                    if last and tile == 0 and RIM <= row + k < RIM + ROWS:
                        pressure_ref[pl.ds(row + k - RIM, CZ, stride=ROWS), :] = value

        return step

    rows_loop(12, 48, 18, smooth(flow, flow_next))
    rows_loop(13, 47, 34, smooth(flow_next, flow, True))

    pressure_copy = pltpu.make_async_copy(pressure_ref, pressure_out, out_sem.at[0])
    pressure_copy.start()

    def finish(row, chunk):
        for k, near in enumerate(near_rows(flow, row, chunk, 1)):
            left_over = rhs(0, row + k) - diag[0, row + k] * state[0, row + k]
            left_over = left_over + get(wet, 0, row + k) * near[0]
            residual_ref[pl.ds(row + k - RIM, CZ, stride=ROWS), :] = left_over

    rows_loop(RIM, RIM + ROWS, 32, finish)
    residual_copy = pltpu.make_async_copy(residual_ref, residual_out, out_sem.at[1])
    residual_copy.start()
    pressure_copy.wait()
    residual_copy.wait()


def swapped(array, axis, first):
    pairs = [(i, i + 1) for i in range(first, lax.axis_size(axis) - 1, 2)]
    return lax.ppermute(array, axis, pairs + [(j, i) for i, j in pairs])


def in_hbm(array):
    return pltpu.with_memory_space_constraint(array, pltpu.HBM)


def f32(*shape):
    return jax.ShapeDtypeStruct(shape, jnp.float32)


def body(right_side, wet_mask, helmholtz, eig_low, eig_high):
    flat = (CZ * ROWS, LANES)
    right_flat = right_side.reshape(flat)
    mask_flat = wet_mask.reshape(flat)
    helm_flat = helmholtz.reshape(flat)
    limits = pltpu.CompilerParams(vmem_limit_bytes=24 * 1024 * 1024)

    far, near, own = pl.pallas_call(
        strips_kernel,
        out_shape=(f32(STRIP, CZ, LANES), f32(STRIP, CZ, LANES), f32(3, ROWS, CZ, LANES)),
        in_specs=[HBM] * 3,
        out_specs=(VMEM,) * 3,
        scratch_shapes=[
            pltpu.VMEM(flat, jnp.int32),
            pltpu.VMEM(flat, jnp.float32),
            pltpu.VMEM(flat, jnp.float32),
            pltpu.SemaphoreType.DMA((3,)),
        ],
        compiler_params=limits,
        name="strips",
    )(in_hbm(right_flat), in_hbm(mask_flat), in_hbm(helm_flat))
    far = swapped(far, "wide", 1)
    near = swapped(near, "wide", 0)

    tall, far, near, eigs = pl.pallas_call(
        sides_kernel,
        out_shape=(
            f32(3, TALL, CZ, LANES),
            f32(3 * PACKED, CZ, LANES),
            f32(3 * PACKED, CZ, LANES),
            f32(2, CZ, LANES),
        ),
        in_specs=[SMEM] * 2 + [VMEM] * 3,
        out_specs=(VMEM,) * 4,
        compiler_params=limits,
        name="sides",
    )(eig_low, eig_high, own, far, near)
    far = swapped(far, "narrow", 1)
    near = swapped(near, "narrow", 0)

    pressure, residual = pl.pallas_call(
        cycle_kernel,
        out_shape=(f32(*flat),) * 2,
        in_specs=[VMEM] * 4,
        out_specs=(HBM,) * 2,
        scratch_shapes=[pltpu.VMEM((2, TALL * PITCH + 2 * CZ, LANES), jnp.float32)] * 3
        + [pltpu.VMEM((TALL, CZ, LANES), jnp.float32)] * 2
        + [pltpu.VMEM((2, TALL, CZ, LANES), jnp.float32)] * 4
        + [pltpu.VMEM((2, TALL // 2 * PITCH + 2 * CZ, LANES), jnp.float32)] * 3
        + [pltpu.VMEM((2, TALL // 2, CZ, LANES), jnp.float32)] * 5
        + [pltpu.VMEM(flat, jnp.float32)] * 2
        + [pltpu.SemaphoreType.DMA((2,))],
        compiler_params=limits,
        name="cycle",
    )(eigs, tall, far, near)
    shape = (CZ, ROWS, LANES)
    return pressure.reshape(shape), residual.reshape(shape)


def solution(mesh):
    field = P(None, "wide", "narrow")
    return jax.shard_map(
        body,
        mesh=mesh,
        in_specs=(field, field, field, P(), P()),
        out_specs=(field, field),
        check_vma=False,
    )
```

```python
import functools

import jax
import jax.numpy as jnp
from jax import lax
from jax.experimental import pallas as pl
from jax.experimental.pallas import tpu as pltpu
from jax.sharding import PartitionSpec as P

CHEB = 4

CZ = 8
ROWS = 32
LANES = 128
RIM = 14
TALL = ROWS + 2 * RIM + 4
MASK_RIM = 13
RIGHT_RIM = 12
STRIP = MASK_RIM + 2 * RIGHT_RIM
SIDE = 16
SPAN = 2 * SIDE
BLOCK = TALL * SPAN // LANES
BLOCKS = LANES // SPAN
PACKED = BLOCK // 2
PITCH = 2 * CZ

VMEM = pl.BlockSpec(memory_space=pltpu.VMEM)
SMEM = pl.BlockSpec(memory_space=pltpu.SMEM)
HBM = pl.BlockSpec(memory_space=pltpu.HBM)


def brick_row(ref, row):
    return ref[pl.ds(row, CZ, stride=ROWS), :]


def strips_kernel(
    right_hbm, mask_hbm, helm_hbm, far_ref, near_ref, own_ref, mask_ref, helm_ref, right_ref, sem
):
    odd = lax.rem(lax.axis_index("wide"), 2)
    copies = [
        pltpu.make_async_copy(source, dest, sem.at[k])
        for k, (source, dest) in enumerate(
            ((mask_hbm, mask_ref), (helm_hbm, helm_ref), (right_hbm, right_ref))
        )
    ]
    for copy in copies:
        copy.start()
    for field, (ref, rim, offset) in enumerate(
        (
            (mask_ref, MASK_RIM, 0),
            (helm_ref, RIGHT_RIM, MASK_RIM),
            (right_ref, RIGHT_RIM, MASK_RIM + RIGHT_RIM),
        )
    ):
        copies[field].wait()
        for row in range(ROWS):
            line = brick_row(ref, row).astype(jnp.float32)
            own_ref[field, row] = line
        to_far, to_near = (ROWS - rim) * odd, (ROWS - rim) * (1 - odd)
        for row in range(rim):
            far_ref[offset + row] = own_ref[field, to_far + row]
            near_ref[offset + row] = own_ref[field, to_near + row]


def sides_kernel(
    low_ref, high_ref, own_ref, far_ref, near_ref, tall_ref, far_out, near_out, eig_ref
):
    odd = lax.rem(lax.axis_index("wide"), 2)
    odd_column = lax.rem(lax.axis_index("narrow"), 2) == 1
    eig_ref[0] = jnp.full((CZ, LANES), low_ref[0], jnp.float32)
    eig_ref[1] = jnp.full((CZ, LANES), high_ref[0], jnp.float32)
    zero = jnp.zeros((CZ, LANES), jnp.float32)
    lane = lax.broadcasted_iota(jnp.int32, (CZ, LANES), 1)
    for field, offset, rim in (
        (0, 0, MASK_RIM),
        (1, MASK_RIM, RIGHT_RIM),
        (2, MASK_RIM + RIGHT_RIM, RIGHT_RIM),
    ):
        for row in (0, 1) + tuple(range(TALL - 6, TALL)):
            tall_ref[field, row] = zero
        from_far = RIM - rim + (ROWS + rim) * odd
        from_near = RIM - rim + (ROWS + rim) * (1 - odd)
        for row in range(rim):
            tall_ref[field, from_far + row] = far_ref[offset + row]
            tall_ref[field, from_near + row] = near_ref[offset + row]
        for row in range(ROWS):
            tall_ref[field, RIM + row] = own_ref[field, row]

    block, half = lane // SPAN, lane & (SPAN - 1) < SIDE

    def pack(start, count):
        for i, field in ((start + k, field) for k in range(count) for field in range(3)):
            first, last = zero, zero
            for b in range(BLOCKS):
                low = tall_ref[field, BLOCK * b + i]
                low = pltpu.roll(low, SPAN * b + SIDE, 1)
                high = tall_ref[field, BLOCK * b + i + BLOCK // 2]
                high = pltpu.roll(high, SPAN * (b + 1), 1) if b + 1 < BLOCKS else high
                here, after = block == b, block == (b + 1) % BLOCKS
                last = jnp.where(here, jnp.where(half, low, high), last)
                first = jnp.where(here & ~half, low, jnp.where(after & half, high, first))
            place = field * PACKED + i
            far_out[place] = jnp.where(odd_column, last, first)
            near_out[place] = jnp.where(odd_column, first, last)

    rows_loop(0, PACKED, 8, pack)


def rows_loop(start, stop, chunk, step):
    count = (stop - start) // chunk
    assert count * chunk == stop - start

    if count == 1:
        step(start, chunk)
        return

    def body(index, carry):
        step(start + index * chunk, chunk)
        return carry

    lax.fori_loop(0, count, body, 0)


def cycle_kernel(
    eig_ref,
    tall_ref,
    far_ref,
    near_ref,
    pressure_out,
    residual_out,
    wet,
    flow,
    flow_next,
    helm_side,
    rhs_side,
    diag,
    base,
    gain,
    state,
    wet_c,
    masked,
    masked_next,
    diag_c,
    inverse_c,
    remain,
    error,
    direction,
    pressure_ref,
    residual_ref,
    out_sem,
):
    lane = lax.broadcasted_iota(jnp.int32, (CZ, LANES), 1)
    level = lax.broadcasted_iota(jnp.int32, (CZ, LANES), 0)
    zero = jnp.zeros((CZ, LANES), jnp.float32)
    tiles = (0, 1)

    def put(ref, tile, row, value):
        ref[tile, pl.ds(row * PITCH + CZ, CZ), :] = value

    def get(ref, tile, row, shift=0):
        return ref[tile, pl.ds(row * PITCH + (CZ + shift), CZ), :]

    def clear(ref, count, reach):
        for place in [CZ - 1 - k for k in range(reach)] + [2 * CZ + k for k in range(reach)]:
            for first in range(0, count, CZ):
                first = min(first, count - CZ)
                for tile in tiles:
                    ref[tile, pl.ds(first * PITCH + place, CZ, stride=PITCH), :] = zero

    for ref in (wet, flow, flow_next):
        clear(ref, TALL, 1)
    for ref in (wet_c, masked, masked_next):
        clear(ref, TALL // 2, 2)

    def beside(main, side, reach):
        low, high = lane < reach, lane >= LANES - reach
        main_up, side_up = pltpu.roll(main, reach, 1), pltpu.roll(side, reach, 1)
        main_down = pltpu.roll(main, LANES - reach, 1)
        side_down = pltpu.roll(side, LANES - reach, 1)
        return (
            (jnp.where(low, side_up, main_up), jnp.where(high, side_down, main_down)),
            (jnp.where(low, main_up, side_up), jnp.where(high, main_down, side_down)),
        )

    def near_rows(ref, row, count, reach):
        lines = [[get(ref, tile, row + k - 1) for tile in tiles] for k in range(2)]
        for k in range(count):
            lines.append([get(ref, tile, row + k + 1) for tile in tiles])
            here = lines[k + 1]
            sides = beside(here[0], here[1], reach)
            yield [
                (lines[k][tile] + lines[k + 2][tile])
                + (get(ref, tile, row + k, -reach) + get(ref, tile, row + k, reach))
                + (sides[tile][0] + sides[tile][1])
                for tile in tiles
            ]

    odd_column = lax.rem(lax.axis_index("narrow"), 2) == 1

    def unpack(start, count):
        edges = (lane < SIDE) | (lane >= LANES - SIDE)
        left_half = lane & (SPAN - 1) < SIDE
        for i, field in ((start + k, field) for k in range(count) for field in range(3)):
            far, near = far_ref[field * PACKED + i], near_ref[field * PACKED + i]
            right = jnp.where(odd_column, far, near)
            left = jnp.where(odd_column, near, far)
            early = jnp.where(left_half, left, right)
            late = jnp.where(left_half, right, left)
            for b in range(BLOCKS):
                low = pltpu.roll(early, LANES - SPAN * b - SIDE, 1)
                high = pltpu.roll(late, LANES - SPAN * (b + 1), 1) if b + 1 < BLOCKS else late
                for row, side in ((BLOCK * b + i, low), (BLOCK * b + i + PACKED, high)):
                    side = jnp.where(edges, side, 0.0)
                    if field == 0:
                        put(wet, 0, row, tall_ref[0, row])
                        put(wet, 1, row, side)
                    else:
                        (helm_side, rhs_side)[field - 1][row] = side

    rows_loop(0, PACKED, 4, unpack)

    def helm(tile, row):
        return helm_side[row] if tile else tall_ref[1, row]

    def rhs(tile, row):
        return rhs_side[row] if tile else tall_ref[2, row]

    def smooth_setup(row, chunk):
        for k, count in enumerate(near_rows(wet, row, chunk, 1)):
            for tile in tiles:
                water = get(wet, tile, row + k)
                scale = water * (helm(tile, row + k) + count[tile]) + (1.0 - water)
                inverse = 0.8 / scale
                start = inverse * rhs(tile, row + k)
                diag[tile, row + k] = scale
                base[tile, row + k] = start
                gain[tile, row + k] = inverse * water
                put(flow, tile, row + k, water * start)

    rows_loop(2, 58, 28, smooth_setup)

    def smooth_second(row, chunk):
        for k, near in enumerate(near_rows(flow, row, chunk, 1)):
            for tile in tiles:
                value = 1.2 * base[tile, row + k] + gain[tile, row + k] * near[tile]
                state[tile, row + k] = value
                put(flow_next, tile, row + k, get(wet, tile, row + k) * value)

    rows_loop(3, 57, 27, smooth_second)

    def pair_sum(value):
        value = value + jnp.where(
            level % 2 == 0, pltpu.roll(value, CZ - 1, 0), pltpu.roll(value, 1, 0)
        )
        return value + jnp.where(
            lane % 2 == 0, pltpu.roll(value, LANES - 1, 1), pltpu.roll(value, 1, 1)
        )

    def coarse_mask(row, chunk):
        for k in range(chunk):
            for tile in tiles:
                fine = 2 * (row + k)
                total = pair_sum(get(wet, tile, fine) + get(wet, tile, fine + 1))
                put(wet_c, tile, row + k, jnp.where(total >= 3.5, 1.0, 0.0))

    rows_loop(1, 29, 14, coarse_mask)

    low, high = eig_ref[0], eig_ref[1]
    centre = 0.5 * (high + low)
    half = 0.5 * (high - low)
    sigma = centre / half
    rho = 1.0 / sigma
    start_scale = 1.0 / centre

    def coarse_setup(row, chunk):
        fine_near = near_rows(flow_next, 2 * row, 2 * chunk, 1)
        for k, count_c in enumerate(near_rows(wet_c, row, chunk, 2)):
            source, shift = [zero, zero], [zero, zero]
            for fine in (2 * (row + k), 2 * (row + k) + 1):
                near = next(fine_near)
                for tile in tiles:
                    left_over = rhs(tile, fine) - diag[tile, fine] * state[tile, fine]
                    source[tile] += get(wet, tile, fine) * (left_over + near[tile])
                    shift[tile] += helm(tile, fine)
            for tile in tiles:
                first_sum = 0.125 * pair_sum(source[tile])
                water_c = get(wet_c, tile, row + k)
                scale = water_c * (0.125 * pair_sum(shift[tile]) + 0.25 * count_c[tile])
                scale = scale + (1.0 - water_c)
                inverse = 1.0 / scale
                first = first_sum * inverse * start_scale
                diag_c[tile, row + k] = scale
                inverse_c[tile, row + k] = inverse
                remain[tile, row + k] = first_sum
                error[tile, row + k] = first
                direction[tile, row + k] = first
                put(masked, tile, row + k, water_c * first)

    rows_loop(2, 28, 13, coarse_setup)

    now, later = masked, masked_next
    for sweep in range(1, CHEB):
        rho_next = 1.0 / (2.0 * sigma - rho)
        keep = rho_next * rho
        add = 2.0 * rho_next / half

        def chebyshev(row, chunk, keep=keep, add=add, now=now, later=later):
            for k, near in enumerate(near_rows(now, row, chunk, 2)):
                for tile in tiles:
                    old = direction[tile, row + k]
                    water_c = get(wet_c, tile, row + k)
                    image = diag_c[tile, row + k] * old - 0.25 * water_c * near[tile]
                    left_over = remain[tile, row + k] - image
                    fresh = keep * old + add * (left_over * inverse_c[tile, row + k])
                    remain[tile, row + k] = left_over
                    direction[tile, row + k] = fresh
                    error[tile, row + k] = error[tile, row + k] + fresh
                    put(later, tile, row + k, water_c * fresh)

        rows_loop(2 + sweep, 28 - sweep, 26 - 2 * sweep, chebyshev)
        rho = rho_next
        now, later = later, now

    def spread(row, chunk):
        for k in range(chunk):
            value = [error[tile, row + k] for tile in tiles]
            sides = beside(value[0], value[1], 1)
            for tile in tiles:
                line = 0.75 * value[tile] + 0.25 * jnp.where(
                    lane % 2 == 0, sides[tile][0], sides[tile][1]
                )
                other = jnp.where(level % 2 == 0, pltpu.roll(line, 1, 0), pltpu.roll(line, CZ - 1, 0))
                other = jnp.where((level == 0) | (level == CZ - 1), 0.0, other)
                direction[tile, row + k] = 0.75 * line + 0.25 * other

    rows_loop(5, 25, 20, spread)

    def correct(row, chunk):
        for k in range(chunk):
            for tile in tiles:
                here = 0.75 * direction[tile, row + k]
                for fine, side in ((2 * (row + k), row + k - 1), (2 * (row + k) + 1, row + k + 1)):
                    water = get(wet, tile, fine)
                    value = state[tile, fine] + water * (here + 0.25 * direction[tile, side])
                    state[tile, fine] = value
                    put(flow, tile, fine, water * value)

    rows_loop(5, 25, 20, correct)

    def smooth(now, later, last=False):
        def step(row, chunk):
            for k, near in enumerate(near_rows(now, row, chunk, 1)):
                for tile in tiles:
                    value = 0.2 * state[tile, row + k] + base[tile, row + k]
                    value = value + gain[tile, row + k] * near[tile]
                    state[tile, row + k] = value
                    put(later, tile, row + k, get(wet, tile, row + k) * value)
                    if last and tile == 0 and RIM <= row + k < RIM + ROWS:
                        pressure_ref[pl.ds(row + k - RIM, CZ, stride=ROWS), :] = value

        return step

    rows_loop(12, 48, 36, smooth(flow, flow_next))
    rows_loop(13, 47, 34, smooth(flow_next, flow, True))

    pressure_copy = pltpu.make_async_copy(pressure_ref, pressure_out, out_sem.at[0])
    pressure_copy.start()

    def finish(row, chunk):
        for k, near in enumerate(near_rows(flow, row, chunk, 1)):
            left_over = rhs(0, row + k) - diag[0, row + k] * state[0, row + k]
            left_over = left_over + get(wet, 0, row + k) * near[0]
            residual_ref[pl.ds(row + k - RIM, CZ, stride=ROWS), :] = left_over

    rows_loop(RIM, RIM + ROWS, 32, finish)
    residual_copy = pltpu.make_async_copy(residual_ref, residual_out, out_sem.at[1])
    residual_copy.start()
    pressure_copy.wait()
    residual_copy.wait()


def swapped(array, axis, first):
    pairs = [(i, i + 1) for i in range(first, lax.axis_size(axis) - 1, 2)]
    return lax.ppermute(array, axis, pairs + [(j, i) for i, j in pairs])


def in_hbm(array):
    return pltpu.with_memory_space_constraint(array, pltpu.HBM)


def f32(*shape):
    return jax.ShapeDtypeStruct(shape, jnp.float32)


def body(right_side, wet_mask, helmholtz, eig_low, eig_high):
    flat = (CZ * ROWS, LANES)
    right_flat = right_side.reshape(flat)
    mask_flat = wet_mask.reshape(flat)
    helm_flat = helmholtz.reshape(flat)
    limits = pltpu.CompilerParams(vmem_limit_bytes=24 * 1024 * 1024)

    far, near, own = pl.pallas_call(
        strips_kernel,
        out_shape=(f32(STRIP, CZ, LANES), f32(STRIP, CZ, LANES), f32(3, ROWS, CZ, LANES)),
        in_specs=[HBM] * 3,
        out_specs=(VMEM,) * 3,
        scratch_shapes=[
            pltpu.VMEM(flat, jnp.int32),
            pltpu.VMEM(flat, jnp.float32),
            pltpu.VMEM(flat, jnp.float32),
            pltpu.SemaphoreType.DMA((3,)),
        ],
        compiler_params=limits,
        name="strips",
    )(in_hbm(right_flat), in_hbm(mask_flat), in_hbm(helm_flat))
    far = swapped(far, "wide", 1)
    near = swapped(near, "wide", 0)

    tall, far, near, eigs = pl.pallas_call(
        sides_kernel,
        out_shape=(
            f32(3, TALL, CZ, LANES),
            f32(3 * PACKED, CZ, LANES),
            f32(3 * PACKED, CZ, LANES),
            f32(2, CZ, LANES),
        ),
        in_specs=[SMEM] * 2 + [VMEM] * 3,
        out_specs=(VMEM,) * 4,
        compiler_params=limits,
        name="sides",
    )(eig_low, eig_high, own, far, near)
    far = swapped(far, "narrow", 1)
    near = swapped(near, "narrow", 0)

    pressure, residual = pl.pallas_call(
        cycle_kernel,
        out_shape=(f32(*flat),) * 2,
        in_specs=[VMEM] * 4,
        out_specs=(HBM,) * 2,
        scratch_shapes=[pltpu.VMEM((2, TALL * PITCH + 2 * CZ, LANES), jnp.float32)] * 3
        + [pltpu.VMEM((TALL, CZ, LANES), jnp.float32)] * 2
        + [pltpu.VMEM((2, TALL, CZ, LANES), jnp.float32)] * 4
        + [pltpu.VMEM((2, TALL // 2 * PITCH + 2 * CZ, LANES), jnp.float32)] * 3
        + [pltpu.VMEM((2, TALL // 2, CZ, LANES), jnp.float32)] * 5
        + [pltpu.VMEM(flat, jnp.float32)] * 2
        + [pltpu.SemaphoreType.DMA((2,))],
        compiler_params=limits,
        name="cycle",
    )(eigs, tall, far, near)
    shape = (CZ, ROWS, LANES)
    return pressure.reshape(shape), residual.reshape(shape)


def solution(mesh):
    field = P(None, "wide", "narrow")
    return jax.shard_map(
        body,
        mesh=mesh,
        in_specs=(field, field, field, P(), P()),
        out_specs=(field, field),
        check_vma=False,
    )
```
